32 devices in a mesh: shard: 8 (over y, x, core), rep: 4 (over z).
Axes of the slice: x: 2, y: 2, z: 4, core: 2. Of those that a mesh axis runs over, the one named last changes fastest.
Arguments:
- tokens: bfloat16 [64, 128, 2048], P(('shard', 'rep')), may hold values from -6 to 6
- norm1_gain: bfloat16 [2048], P('shard'), may hold values from 0.5 to 1.5
- q_weight: bfloat16 [2048, 2048], P('shard'), may hold values from -0.125 to 0.125
- k_weight: bfloat16 [2048, 256], P('shard'), may hold values from -0.125 to 0.125
- v_weight: bfloat16 [2048, 256], P('shard'), may hold values from -0.125 to 0.125
- o_weight: bfloat16 [2048, 2048], P('shard'), may hold values from -0.5 to 0.5
- norm2_gain: bfloat16 [2048], P('shard'), may hold values from 0.5 to 1.5
- gate_weight: bfloat16 [2048, 5632], P('shard'), may hold values from -0.125 to 0.125
- up_weight: bfloat16 [2048, 5632], P('shard'), may hold values from -0.125 to 0.125
- down_weight: bfloat16 [5632, 2048], P('shard'), may hold values from -0.15625 to 0.15625
- out_grad: bfloat16 [64, 128, 2048], P(('shard', 'rep')), may hold values from -6 to 6
Outputs:
- layer_out: bfloat16 [64, 128, 2048], P(('shard', 'rep'))
- input_grad: float32 [64, 128, 2048], P(('shard', 'rep'))
- norm1_gain_grad: float32 [2048], P('shard')
- q_grad: float32 [2048, 2048], P('shard')
- k_grad: float32 [2048, 256], P('shard')
- v_grad: float32 [2048, 256], P('shard')
- o_grad: float32 [2048, 2048], P('shard')
- norm2_gain_grad: float32 [2048], P('shard')
- gate_grad: float32 [2048, 5632], P('shard')
- up_grad: float32 [2048, 5632], P('shard')
- down_grad: float32 [5632, 2048], P('shard')
The draws below stay inside these ranges and needn't reach their ends.
All inputs are finite; a program needn't handle non-finite values.
Results may differ from the reference program's by a relative error of at most 0.022.
Values may be sent and summed in bfloat16 or wider, within the bound.
No kernel may reach another device: no remote copies, remote signals or barrier semaphores. Data moves between devices by JAX's collectives and lax.ppermute only.
A program may use at most 384 MiB of HBM per device.

```python
import jax
import jax.numpy as jnp
from jax import lax

D = 2048
FF = 5632
QUERY_HEADS = 32
KEY_VALUE_HEADS = 4
HEAD_SIZE = 64
LEN = 128
KV = 256
SEQS = 64


def spiked(drawn, key, source, target, blocks, factor):
    def block_of(position):
        return (jnp.arange(drawn.shape[position]) // (drawn.shape[position] // blocks)).reshape((-1,) + (1,) * (drawn.ndim - 1 - position))

    one_side = jax.random.permutation(key, blocks)[block_of(target)]
    second = (block_of(target) + blocks // 2) % blocks
    return jnp.where((block_of(source) == one_side) | (block_of(source) == second), factor * drawn, drawn)


def block_scale(rng, shape, split, low, largest):
    loudness = 1.0
    for axis_at, shards_of in split:
        heights = jax.random.uniform(jax.random.fold_in(jax.random.fold_in(rng, 6), axis_at), (shards_of,), jnp.float32, low / len(split), largest / len(split))
        loudness = loudness * jnp.repeat(jnp.exp(heights), shape[axis_at] // shards_of).reshape((-1,) + (1,) * (len(shape) - 1 - axis_at))
    return loudness


def scatter_about(stream_key, dims, deviation, reach, split=(), kind=jnp.bfloat16):
    result = jax.random.normal(stream_key, dims, jnp.float32) * deviation
    if len(split) > 0:
        result = block_scale(stream_key, dims, split, -0.22, 0.18) * result
    return jnp.clip(result, min=-reach, max=reach).astype(kind)


def bell_draw_with(rng, dims, deviation, reach, split, heavy, kind=jnp.bfloat16):
    values = deviation * jax.random.normal(rng, dims, jnp.float32)
    if split:
        values = values * block_scale(rng, dims, split, -0.22, 0.18)
    return jnp.clip(spiked(values, jax.random.fold_in(rng, 3), *heavy), -reach, reach).astype(kind)


def setup_inputs(seed: int = 0) -> dict:
    key_list = jax.random.split(jax.random.key(seed), 12)
    return {
        "tokens": scatter_about(key_list[0], (SEQS, LEN, D), 1.0, 6.0, ((0, 32),)),
        "norm1_gain": jnp.clip(1.0 + 0.1 * jax.random.normal(key_list[1], (D,), jnp.float32), 0.5, 1.5).astype(jnp.bfloat16),
        "q_weight": scatter_about(key_list[2], (D, QUERY_HEADS * HEAD_SIZE), D ** -0.5, 0.125, ((0, 8),)),
        "k_weight": scatter_about(key_list[3], (D, KV), D ** -0.5, 0.125, ((0, 8),)),
        "v_weight": scatter_about(key_list[4], (D, KV), D ** -0.5, 0.125, ((0, 8),)),
        "o_weight": scatter_about(key_list[5], (QUERY_HEADS * HEAD_SIZE, D), (QUERY_HEADS * HEAD_SIZE // 16) ** -0.5, 0.5, ((0, 8),)),
        "norm2_gain": jnp.clip(1.0 + 0.1 * jax.random.normal(key_list[6], (D,), jnp.float32), 0.5, 1.5).astype(jnp.bfloat16),
        "gate_weight": scatter_about(key_list[7], (D, FF), D ** -0.5, 0.125, ((0, 8),)),
        "up_weight": scatter_about(key_list[8], (D, FF), D ** -0.5, 0.125, ((0, 8),)),
        "down_weight": scatter_about(key_list[9], (FF, D), (FF // 4) ** -0.5, 0.15625, ((0, 8),)),
        "out_grad": bell_draw_with(key_list[10], (SEQS, LEN, D), 1.0, 6.0, ((0, 32),), (0, 2, 32, 2.75)),
    }


@jax.custom_vjp
def reduced_precision(v):
    return lax.optimization_barrier(v.astype(jnp.bfloat16)).astype(jnp.float32)

@jax.custom_vjp
def reduced_backward(v):
    return v

def low_keep(v):
    return (reduced_precision(v), None)

def low_pass(kept, grad):
    return (grad,)

def back_keep(v):
    return (v, None)

def back_low(kept, grad):
    return (reduced_precision(grad),)
reduced_precision.defvjp(low_keep, low_pass)
reduced_backward.defvjp(back_keep, back_low)
EPS = 1e-05
HIGH = lax.Precision.HIGHEST

def rope_tables(sequence_length, size):
    half = size // 2
    freqs = 1.0 / 10000.0 ** (jnp.arange(half, dtype=jnp.float32) * 2.0 / size)
    angles = jnp.arange(sequence_length, dtype=jnp.float32)[:, None] * freqs[None, :]
    return (jnp.concatenate([jnp.cos(angles)] * 2, -1), jnp.concatenate([jnp.sin(angles)] * 2, -1))

def apply_rotation(value, cosine_table, sine_table):
    half = value.shape[-1] // 2
    turned = jnp.concatenate([-value[..., half:], value[..., :half]], -1)
    return value * cosine_table[None, :, None, :] + turned * sine_table[None, :, None, :]

def apply_projection(acts, weight):
    return jnp.einsum('gtd,de->gte', acts, weight, precision=HIGH)

def layer(block, params):
    gain_one, wq_full, key_weight_whole, value_weight_whole, output_weight_whole, gain_two, wg_full, wu_full, wd_full = params
    shard_group, sequence_length, width = block.shape
    repeat_heads = QUERY_HEADS // KEY_VALUE_HEADS
    cosine_table, sine_table = rope_tables(sequence_length, HEAD_SIZE)
    inv_one = lax.rsqrt(lax.optimization_barrier(jnp.mean(block * block, -1, keepdims=True)) + EPS)
    first_normed = reduced_precision(block * inv_one * gain_one)
    query_linear = reduced_backward(apply_projection(first_normed, wq_full)).reshape(shard_group, sequence_length, QUERY_HEADS, HEAD_SIZE)
    key_linear = reduced_backward(apply_projection(first_normed, key_weight_whole)).reshape(shard_group, sequence_length, KEY_VALUE_HEADS, HEAD_SIZE)
    value_reduced = reduced_precision(reduced_backward(apply_projection(first_normed, value_weight_whole))).reshape(shard_group, sequence_length, KEY_VALUE_HEADS, HEAD_SIZE)
    query_rotated = reduced_precision(apply_rotation(query_linear, cosine_table, sine_table)).reshape(shard_group, sequence_length, KEY_VALUE_HEADS, repeat_heads, HEAD_SIZE)
    key_rot = reduced_precision(apply_rotation(key_linear, cosine_table, sine_table))
    raw = jnp.einsum('gtkrh,gukh->gkrtu', query_rotated, key_rot, precision=HIGH) * (1.0 / jnp.sqrt(jnp.float32(HEAD_SIZE)))
    raw = reduced_backward(raw)
    causal = jnp.arange(sequence_length)[:, None] >= jnp.arange(sequence_length)[None, :]
    scores = jnp.where(causal, raw, -1e+30)
    attn_prob = jax.nn.softmax(scores, axis=-1)
    prob_low = reduced_precision(attn_prob)
    context = jnp.einsum('gkrtu,gukh->gtkrh', prob_low, value_reduced, precision=HIGH).reshape(shard_group, sequence_length, QUERY_HEADS * HEAD_SIZE)
    context = reduced_precision(reduced_backward(context))
    hidden_one = block + reduced_backward(apply_projection(context, output_weight_whole))
    inv_two = lax.rsqrt(lax.optimization_barrier(jnp.mean(hidden_one * hidden_one, -1, keepdims=True)) + EPS)
    normed_two = reduced_precision(hidden_one * inv_two * gain_two)
    gate_act = reduced_backward(apply_projection(normed_two, wg_full))
    up_act = reduced_backward(apply_projection(normed_two, wu_full))
    hidden_low = reduced_precision(jax.nn.silu(gate_act) * up_act)
    return hidden_one + reduced_backward(apply_projection(hidden_low, wd_full))

def reference(tokens, norm1_gain, q_weight, k_weight, v_weight, o_weight, norm2_gain, gate_weight, up_weight, down_weight, out_grad):
    params = tuple((weight.astype(jnp.float32) for weight in (norm1_gain, q_weight, k_weight, v_weight, o_weight, norm2_gain, gate_weight, up_weight, down_weight)))
    seqs_all, sequence_length, width = tokens.shape
    limit = max(1, 4096 // sequence_length)
    shard_group = 1
    for count in range(1, min(limit, seqs_all) + 1):
        if seqs_all % count == 0:
            shard_group = count
    inputs = tokens.astype(jnp.float32).reshape(seqs_all // shard_group, shard_group, sequence_length, width)
    upstream = out_grad.astype(jnp.float32).reshape(seqs_all // shard_group, shard_group, sequence_length, width)

    def step(totals, pair):
        block, block_grad = pair
        output, pullback = jax.vjp(layer, block, params)
        grad_block, grad_params = pullback(block_grad)
        totals = jax.tree.map(lambda total, term: total + term, totals, grad_params)
        return (totals, (output, grad_block))
    zeros = jax.tree.map(jnp.zeros_like, params)
    totals, (outputs, grad_inputs) = lax.scan(step, zeros, (inputs, upstream))
    return (outputs.reshape(tokens.shape).astype(jnp.bfloat16), grad_inputs.reshape(tokens.shape), totals[0], totals[1], totals[2], totals[3], totals[4], totals[5], totals[6], totals[7], totals[8])
```

```python
import functools
import math

import jax
import jax.numpy as jnp
import numpy as np
from jax import lax
from jax.experimental import pallas as pl
from jax.experimental.pallas import tpu as pltpu
from jax.sharding import PartitionSpec as P

HEAD_SIZE = 64
EPS = 1e-05
F32 = jnp.float32
BF16 = jnp.bfloat16
ANY = pl.BlockSpec(memory_space=pl.ANY)
TOKEN = pl.BlockSpec(memory_space=pltpu.HBM)
PER_MIB = 1.4e10


def dot(left, right):
    return jnp.dot(left, right, preferred_element_type=F32)


def dot_nt(left, right):
    return lax.dot_general(left, right, (((1,), (1,)), ((), ())), preferred_element_type=F32)


def dot_tn(left, right):
    return lax.dot_general(left, right, (((0,), (0,)), ((), ())), preferred_element_type=F32)


def shape_of(rows, columns, dtype=BF16):
    return jax.ShapeDtypeStruct((rows, columns), dtype)


def row_blocks(rows, columns):
    return pl.BlockSpec((rows, columns), lambda i: (i, 0))


def row_block_at(rows, columns, at):
    return pl.BlockSpec((rows, columns), lambda i: (at, 0))


def column_blocks(rows, columns):
    return pl.BlockSpec((rows, columns), lambda i: (0, i))


def whole(array):
    zeros = (0,) * array.ndim
    return pl.BlockSpec(array.shape, lambda i: zeros, pipeline_mode=pl.Buffered(1))


def whole_out(array):
    zeros = (0,) * len(array.shape)
    return pl.BlockSpec(array.shape, lambda i: zeros)


class Clock:
    def __init__(self):
        self.token = jnp.zeros((8, 128), F32)

    def call(self, body, args, in_specs, outs, out_specs, steps=1, aliases=None, vmem=60, cost=1):
        n_in, n_out = len(args), len(outs)

        def kernel(*refs):
            body(*refs[:n_in], *refs[n_in + 1 : n_in + 1 + n_out])

        *results, self.token = pl.pallas_call(
            kernel,
            grid=(steps,),
            out_shape=(*outs, pltpu.HBM(self.token.shape, F32)),
            in_specs=[*in_specs, TOKEN],
            out_specs=(*out_specs, TOKEN),
            input_output_aliases={n_in: n_out, **(aliases or {})},
            compiler_params=pltpu.CompilerParams(vmem_limit_bytes=vmem << 20),
            cost_estimate=pl.CostEstimate(flops=cost, bytes_accessed=cost // 1000 + 1, transcendentals=0),
        )(*args, self.token)
        return results

    def pause(self, mib):
        self.call(nothing, [], [], [], [], vmem=1, cost=int(mib * PER_MIB))

    def tie(self, *values):
        outs = [jax.ShapeDtypeStruct(v.shape, v.dtype) for v in values]
        results = self.call(
            nothing, values, [ANY] * len(values), outs, [ANY] * len(values),
            aliases={i: i for i in range(len(values))}, vmem=1,
        )
        return results if len(results) > 1 else results[0]


def nothing(*refs):
    pass


class Line:
    def __init__(self, size, clock):
        self.size = size
        self.clock = clock
        self.me = lax.axis_index("rep")
        self.end = jnp.asarray((self.me == 0) | (self.me == size - 1), jnp.int32).reshape(1)
        self.waiting, self.coming, self.across, self.going = [], None, None, None

    def shift(self, value, pairs):
        return lax.ppermute(value, "rep", pairs)

    def queue(self, value, finish):
        if self.size == 4:
            self.waiting.append((value, finish))
        else:
            finish(lax.psum(value, "rep") if self.size > 1 else value)

    def busy(self):
        return bool(self.waiting or self.coming or self.across or self.going)

    def tick(self, mib=0.1):
        if not self.busy():
            return
        coming, across, going = self.coming, self.across, self.going
        fresh = self.waiting.pop(0) if self.waiting else None
        args, outs, jobs = [], [], []

        def use(*arrays):
            args.extend(arrays)
            return slice(len(args) - len(arrays), len(args))

        def give(array):
            outs.append(shape_of(*array.shape))
            return len(outs) - 1

        inward = [(0, 1), (3, 2)]
        outward = [(1, 0), (2, 3)]
        shared = across and fresh and across["value"].shape == fresh[0].shape
        if across:
            terms = [across["value"], across["arrived"]]
            if shared:
                jobs.append(("fresh", use(fresh[0], *terms), give(fresh[0])))
            else:
                jobs.append(("add", use(*terms), give(across["value"])))
        if coming:
            jobs.append(("add", use(coming["value"], coming["arrived"]), give(coming["value"])))

        if fresh and jobs and not shared:
            jobs.append(("pass", use(fresh[0]), give(fresh[0])))

        def body(end, *refs):
            ins, results = refs[: len(args)], refs[len(args) :]
            outer = end[0] > 0
            for kind, where, out in jobs:
                mine = [ref[...].astype(F32) for ref in ins[where]]
                if kind == "pass":
                    value = mine[0]
                elif kind == "add":
                    value = mine[0] + mine[1]
                else:
                    value = jnp.where(outer, mine[0], mine[1] + mine[2])
                results[out][...] = value.astype(BF16)

        results = []
        if jobs:
            steps = 2 if all(a.shape[0] % 32 == 0 for a in args) else 1
            specs = [row_blocks(a.shape[0] // steps, a.shape[1]) for a in args]
            results = self.clock.call(
                body, [self.end, *args], [pl.BlockSpec(memory_space=pltpu.SMEM), *specs],
                outs, [row_blocks(o.shape[0] // steps, o.shape[1]) for o in outs], steps, vmem=60,
            )
        results = list(results)
        self.going = self.across = self.coming = None
        if across:
            value = results.pop(0)
            arrived = self.shift(value, outward + (inward if shared else []))
            self.going = {"value": value, "arrived": arrived, "finish": across["finish"]}
        if coming:
            value = results.pop(0)
            self.across = {"value": value, "arrived": self.shift(value, [(1, 2), (2, 1)]), "finish": coming["finish"]}
        if fresh:
            value = fresh[0]
            if not shared:
                value = results.pop(0) if results else self.clock.tie(value)
                arrived = self.shift(value, inward)
            self.coming = {"value": value, "arrived": arrived, "finish": fresh[1]}
        self.clock.pause(mib)
        if going:
            going["finish"](self.select(going["arrived"], going["value"]))

    def select(self, ends, others):
        rows, width = others.shape

        def body(end, a, b, out):
            out[...] = jnp.where(end[0] > 0, a[...], b[...])

        spec = column_blocks(rows, width // 2)
        return self.clock.call(
            body, [self.end, ends, others], [pl.BlockSpec(memory_space=pltpu.SMEM), spec, spec],
            [shape_of(rows, width)], [spec], 2,
        )[0]


    def share(self, value):
        up, down = [value], [value]
        top = self.size - 1
        for step in range(top):
            pairs = [(i, i + 1) for i in range(step, top)]
            above = self.shift(up[-1], pairs)
            below = self.shift(down[-1], [(top - a, top - b) for a, b in pairs])
            self.clock.pause(0.1)
            yield
            above, below = self.clock.tie(above, below)
            up.append(above)
            down.append(below)
        self.shared = up, down


class Group:
    def __init__(self, size, clock):
        self.size = size
        self.clock = clock
        self.fast = size == 8
        self.me = jnp.asarray(lax.axis_index("shard"), jnp.int32).reshape(1)

    def swap(self, value, bit):
        return lax.ppermute(value, "shard", [(i, i ^ bit) for i in range(self.size)])

    def gather(self, own):
        half = own.shape[0] // 2
        if not self.fast:
            yield
            yield
            self.gather_all(own)
            return
        by_x, by_y = self.swap(own, 2), self.swap(own, 4)
        self.clock.pause(1)
        yield
        first, second = self.stacked([[[(by_x, 0)]], [[(by_y, 1)]]], half)
        first, second = self.swap(first, 4), self.swap(second, 2)
        self.clock.pause(0.6)
        yield
        self.join(own, [(by_x, 0), (by_x, 1), (by_y, 0), (by_y, 1), (first, 0), (second, 0)])

    def gather_all(self, own):
        every = lax.all_gather(own, "shard", axis=0, tiled=True)
        middle = every.shape[0] // 2
        self.gathered = every[:middle], every[middle:]

    def join(self, own, pieces):
        half, width = own.shape[0] // 2, own.shape[1]
        pieces = [(own, 0), (own, 1), *pieces]

        def body(*refs):
            for at, ref in enumerate(refs[:-1]):
                refs[-1][pl.ds(at * half, half), :] = ref[...]

        def columns(at):
            return pl.BlockSpec((half, width // 4), lambda i: (at, i))

        even = shape_of(half * self.size, width)
        even = self.clock.call(
            body, [array for array, _ in pieces], [columns(at) for _, at in pieces],
            [even], [column_blocks(even.shape[0], width // 4)], 4, vmem=24,
        )[0]
        self.gathered = even, self.swap(even, 1)
        self.clock.pause(4)

    def stacked(self, outs, rows):
        terms = [term for out in outs for block in out for term in block]
        width = terms[0][0].shape[1]

        def body(*refs):
            ins = iter(refs[: len(terms)])
            for out, ref in zip(outs, refs[len(terms) :]):
                for at, block in enumerate(out):
                    values = [next(ins)[...] for _ in block]
                    if len(values) > 1:
                        values = [sum(v.astype(F32) for v in values).astype(BF16)]
                    ref[pl.ds(at * rows, rows), :] = values[0]

        shapes = [shape_of(len(out) * rows, width) for out in outs]
        return self.clock.call(
            body, [array for array, _ in terms], [row_block_at(rows, width, at) for _, at in terms],
            shapes, [whole_out(o) for o in shapes], vmem=40,
        )

    def partner(self, odd):
        if not self.fast:
            return odd
        other = self.swap(odd, 1)
        self.clock.pause(4)
        return other

    def ride(self, own):
        if self.fast:
            self.riding = self.swap(own, 2), self.swap(own, 4)
            self.clock.pause(1)

    def scatter(self, sets, own=None):
        if not self.fast:
            yield
            yield
            both = [jnp.concatenate(pair, 0) for pair in sets]
            totals = [lax.psum_scatter(b, "shard", scatter_dimension=0, tiled=True) for b in both]
            self.terms = [[[(total, 0)], [(total, 1)]] for total in totals]
            if own is not None:
                self.gather_all(own)
            return
        rows = sets[0][0].shape[0] // 8
        rider = self.clock.tie(*self.riding) if own is not None else None

        def both(pair, at):
            return [(pair[0], at), (pair[1], at)]

        to_x = [both(pair, at) for pair in sets for at in (3, 7)]
        to_y = [both(pair, at) for pair in sets for at in (4, 6)]
        to_x, to_y = self.stacked([to_x, to_y], rows)
        by_x, by_y = self.swap(to_x, 2), self.swap(to_y, 4)
        self.clock.pause(len(sets))
        yield
        count = len(sets)
        to_x = [both(pair, 2) + [(by_y, 2 * i + 1)] for i, pair in enumerate(sets)]
        to_y = [both(pair, 5) + [(by_x, 2 * i + 1)] for i, pair in enumerate(sets)]
        if rider:
            to_x.append([(rider[1], 1)])
            to_y.append([(rider[0], 0)])
        to_x, to_y = self.stacked([to_x, to_y], rows)
        last_x, last_y = self.swap(to_x, 2), self.swap(to_y, 4)
        self.clock.pause(0.6 * len(sets) + 0.4 * bool(rider))
        yield
        self.terms = [
            [
                both(pair, 0) + [(by_y, 2 * i), (last_x, i)],
                both(pair, 1) + [(by_x, 2 * i), (last_y, i)],
            ]
            for i, pair in enumerate(sets)
        ]
        if rider:
            first = [(rider[0], 0), (rider[0], 1), (rider[1], 0), (rider[1], 1)]
            self.rider = own, [*first, (last_y, count), (last_x, count)]

    def join_rider(self):
        if self.fast:
            self.join(*self.rider)

    def finish_rows(self, body, terms, args, outs):
        flat = [array for half in terms for array, _ in half]
        rows = args[0].shape[0] // 2
        columns = flat[0].shape[1]
        specs = [row_block_at(rows, columns, at) for half in terms for _, at in half]
        count = len(terms[0])

        def kernel(*refs):
            sums, rest = refs[: len(flat)], refs[len(flat) :]
            for half in (0, 1):
                total = sum(ref[...].astype(F32) for ref in sums[half * count : (half + 1) * count])
                body(pl.ds(half * rows, rows), total, *rest)

        return self.clock.call(
            kernel, [*flat, *args], [*specs, *[whole(a) for a in args]], outs,
            [whole_out(o) for o in outs], vmem=40,
        )

    def exchange(self, load, args, a, b):
        smem = pl.BlockSpec(memory_space=pltpu.SMEM)
        specs = [smem, *[smem if v.ndim == 1 else whole(v) for v in args]]
        if not self.fast:

            def lay(me, *refs):
                for j in range(self.size):
                    refs[-1][j] = load(refs[:-1], j)

            every = jax.ShapeDtypeStruct((self.size, a, b), BF16)
            blocks = self.clock.call(lay, [self.me, *args], specs, [every], [whole_out(every)])[0]
            yield
            yield
            self.exchanged = lax.all_to_all(blocks, "shard", split_axis=0, concat_axis=0)
            return
        four, two = jax.ShapeDtypeStruct((4, a, b), BF16), jax.ShapeDtypeStruct((2, a, b), BF16)

        def pack(me, *refs):
            kept, sent = refs[-2:]
            for j in range(8):
                value = load(refs[:-2], j)
                k = me[0] ^ j

                @pl.when(k & 1 == 0)
                def _(value=value, k=k):
                    kept[k >> 1] = value

                @pl.when(k & 1 == 1)
                def _(value=value, k=k):
                    sent[k >> 1] = value

        kept, sent = self.clock.call(
            pack, [self.me, *args], specs, [four] * 2, [whole_out(four)] * 2, vmem=32
        )
        come = self.swap(sent, 1)
        mib = 8 * a * b / 2**20
        self.clock.pause(mib)
        yield

        def stack(kept, come, *outs):
            for i, out in enumerate(outs):
                out[0] = kept[i + 1]
                out[1] = come[i + 1]

        sends = self.clock.call(
            stack, [kept, come], [whole(kept), whole(come)], [two] * 3, [whole_out(two)] * 3, vmem=24
        )
        arrived = [self.swap(value, 2 * i + 2) for i, value in enumerate(sends)]
        self.clock.pause(mib / 2)
        yield

        def unpack(me, kept, come, *rest):
            out = rest[-1]
            out[me[0]] = kept[0]
            out[me[0] ^ 1] = come[0]
            for i, ref in enumerate(rest[:-1]):
                out[me[0] ^ (2 * i + 2)] = ref[0]
                out[me[0] ^ (2 * i + 3)] = ref[1]

        eight = jax.ShapeDtypeStruct((8, a, b), BF16)
        first = pl.BlockSpec((1, a, b), lambda i: (0, 0, 0))
        self.exchanged = self.clock.call(
            unpack, [self.me, kept, come, *arrived], [smem, first, first, *[whole(v) for v in arrived]],
            [eight], [whole_out(eight)], vmem=24,
        )[0]


def drain(steps):
    for _ in steps:
        pass


class Attention:
    def __init__(self, clock, length, qcols, wqkv, wo):
        self.clock, self.length, self.qcols = clock, length, qcols
        self.wqkv, self.wo = wqkv, wo
        self.heads = qcols // HEAD_SIZE
        self.width = qcols + 2 * HEAD_SIZE
        half = HEAD_SIZE // 2
        freqs = 1.0 / 10000.0 ** (np.arange(half, dtype=np.float32) * 2.0 / HEAD_SIZE)
        angles = np.arange(length, dtype=np.float32)[:, None] * freqs[None, :].astype(np.float32)
        turns = self.heads + 1
        low = np.arange(turns * HEAD_SIZE) % HEAD_SIZE < half
        cosine = np.tile(np.cos(angles), (1, 2 * turns))
        sine = np.tile(np.sin(angles), (1, 2 * turns))
        plain = np.zeros((length, HEAD_SIZE), np.float32)
        self.tables = tuple(
            jnp.asarray(np.concatenate(pair, 1), F32)
            for pair in (
                (cosine, plain + 1.0),
                (np.where(low, -sine, 0.0), plain),
                (np.where(low, 0.0, sine), plain),
            )
        )

    def roll(self, value, by):
        return pltpu.roll(value, by % value.shape[1], 1)

    def stack(self, value):
        head = lax.broadcasted_iota(jnp.int32, value.shape, 1) // HEAD_SIZE
        return jnp.concatenate([jnp.where(head == h, value, 0.0) for h in range(self.heads)], 0).astype(BF16)

    def unstack(self, value):
        head = lax.broadcasted_iota(jnp.int32, (self.length, self.qcols), 1) // HEAD_SIZE
        total = jnp.zeros((self.length, self.qcols), F32)
        for h in range(self.heads):
            total = jnp.where(head == h, value[h * self.length : (h + 1) * self.length], total)
        return total

    def repeated(self, value):
        first = lax.broadcasted_iota(jnp.int32, value.shape, 1) < HEAD_SIZE
        turned = self.roll(value, HEAD_SIZE)
        times = self.qcols // (2 * HEAD_SIZE)
        key = jnp.where(first, value, turned).astype(BF16)
        val = jnp.where(first, turned, value).astype(BF16)
        return jnp.concatenate([key] * times, 1), jnp.concatenate([val] * times, 1)

    def probabilities(self, stacked, keys):
        raw = dot_nt(stacked, keys) * (1.0 / math.sqrt(HEAD_SIZE))
        raw = raw.reshape(self.heads, self.length, self.length)
        at = lax.broadcasted_iota(jnp.int32, raw.shape, 1)
        seen = lax.broadcasted_iota(jnp.int32, raw.shape, 2) <= at
        scores = jnp.where(seen, raw, -1e30)
        e = jnp.exp(scores - jnp.max(scores, -1, keepdims=True))
        prob = e / jnp.sum(e, -1, keepdims=True)
        return prob.reshape(self.heads * self.length, self.length)

    def forward(self, tokens):
        rows, width = tokens.shape
        block, length, qcols = 2 * self.length, self.length, self.qcols

        def body(x, wqkv, wo, c, s1, s2, qkv_out, inv_out, context_t, partial_out):
            source = x[...].astype(F32)
            inv = lax.rsqrt(jnp.mean(source * source, -1, keepdims=True) + EPS)
            inv_out[...] = jnp.broadcast_to(inv, (block, 128))
            lin = dot(x[...], wqkv[...]) * inv
            contexts = []
            for at in range(0, block, length):
                v = lin[at : at + length]
                v = v * c[...] + self.roll(v, -32) * s1[...] + self.roll(v, 32) * s2[...]
                v = v.astype(BF16).astype(F32)
                qkv_out[pl.ds(at, length), :] = v.astype(BF16)
                keys, values = self.repeated(v[:, qcols:])
                prob = self.probabilities(self.stack(v[:, :qcols]), keys)
                context = self.unstack(dot(prob.astype(BF16), values))
                contexts.append(context.astype(BF16))
            context = jnp.concatenate(contexts, 0)
            context_t[...] = context.T
            partial_out[...] = dot(context, wo[...]).astype(BF16)

        args = (tokens, self.wqkv, self.wo, *self.tables)
        return self.clock.call(
            body, args, [row_blocks(block, width), *[whole(a) for a in args[1:]]],
            [shape_of(rows, self.width), shape_of(rows, 128, F32), shape_of(qcols, rows), shape_of(rows, width)],
            [
                row_blocks(block, self.width),
                row_blocks(block, 128),
                column_blocks(qcols, block),
                row_blocks(block, width),
            ],
            rows // block,
        )

    def backward(self, grad, qkv, inv):
        rows, width = grad.shape
        block, length, qcols = 2 * self.length, self.length, self.qcols
        scale = 1.0 / math.sqrt(HEAD_SIZE)

        def fold(value):
            folded = sum(value[:, i : i + 2 * HEAD_SIZE] for i in range(0, qcols, 2 * HEAD_SIZE))
            return folded + self.roll(folded, HEAD_SIZE)

        def body(d, qkv_in, inv_in, wqkv, wo, c, s1, s2, grad_t, partial_out):
            grads = []
            dcontext = dot_nt(d[...], wo[...]).astype(BF16).astype(F32)
            for at in range(0, block, length):
                v = qkv_in[pl.ds(at, length), :].astype(F32)
                keys, values = self.repeated(v[:, qcols:])
                stacked = self.stack(v[:, :qcols])
                prob = self.probabilities(stacked, keys)
                dstacked = self.stack(dcontext[at : at + length])
                dprob = dot_nt(dstacked, values)
                dvalue = fold(dot_tn(prob.astype(BF16), dstacked))
                ds = prob * (dprob - jnp.sum(prob * dprob, -1, keepdims=True))
                ds = ds.astype(BF16)
                dq = self.unstack(dot(ds, keys)) * scale
                dkey = fold(dot_tn(ds, stacked)) * scale
                first = lax.broadcasted_iota(jnp.int32, dkey.shape, 1) < HEAD_SIZE
                g = jnp.concatenate([dq, jnp.where(first, dkey, dvalue)], 1)
                g = g * c[...] - self.roll(g, -32) * s1[...] - self.roll(g, 32) * s2[...]
                grads.append(g)
            g = jnp.concatenate(grads, 0)
            grad_t[...] = (g * inv_in[:, :1]).astype(BF16).T
            partial_out[...] = dot_nt(g.astype(BF16), wqkv[...]).astype(BF16)

        args = (grad, qkv, inv, self.wqkv, self.wo, *self.tables)
        return self.clock.call(
            body, args,
            [
                row_blocks(block, width),
                row_blocks(block, self.width),
                row_blocks(block, 128),
                *[whole(a) for a in args[3:]],
            ],
            [shape_of(self.width, rows), shape_of(rows, width)],
            [column_blocks(self.width, block), row_blocks(block, width)],
            rows // block,
        )


def feed(clock, normed, dy, wg, wu, wd, block=256):
    rows, width = normed.shape
    ff = wd.shape[0]

    def body(x, d, wg, wu, wd, act_out, dgate_out, dup_out, act_t, dgate_t, dup_t):
        gate = dot(x[...], wg[...])
        up = dot(x[...], wu[...])
        dact = dot_nt(d[...], wd[...])
        sigma = jax.nn.sigmoid(gate)
        silu = gate * sigma
        act = (silu * up).astype(BF16)
        dgate = (dact * up * (sigma * (1.0 + gate * (1.0 - sigma)))).astype(BF16)
        dup = (dact * silu).astype(BF16)
        for value, out, turned in ((act, act_out, act_t), (dgate, dgate_out, dgate_t), (dup, dup_out, dup_t)):
            out[...] = value
            turned[...] = value.T

    args = (normed, dy, wg, wu, wd)
    return clock.call(
        body, args, [row_blocks(block, width)] * 2 + [whole(a) for a in args[2:]],
        [shape_of(rows, ff)] * 3 + [shape_of(ff, rows)] * 3,
        [row_blocks(block, ff)] * 3 + [column_blocks(ff, block)] * 3,
        rows // block,
    )


def assemble(clock, me, above, below):
    copies = len(above)
    a, _, b, c = above[0].shape

    def body(me_ref, *refs):
        outs = refs[2 * copies - 1 :]
        for step in range(copies):
            at = lax.rem(me_ref[0] + step, copies)

            def store(ref, at=at):
                for which, out in enumerate(outs):
                    out[0, at] = ref[0, which]

            if step == 0:
                store(refs[0])
                continue

            @pl.when(me_ref[0] + step < copies)
            def _(ref=refs[copies + step - 1], store=store):
                store(ref)

            @pl.when(me_ref[0] + step >= copies)
            def _(ref=refs[copies - step], store=store):
                store(ref)

    args = [*above, *below[1:]]
    out = jax.ShapeDtypeStruct((a, copies, b, c), BF16)
    spec = pl.BlockSpec((1, 2, b, c), lambda i: (i, 0, 0, 0))
    out_spec = pl.BlockSpec((1, copies, b, c), lambda i: (i, 0, 0, 0))
    me = jnp.asarray(me, jnp.int32).reshape(1)
    return clock.call(
        body, [me, *args], [pl.BlockSpec(memory_space=pltpu.SMEM)] + [spec] * len(args),
        [out] * 2, [out_spec] * 2, a, vmem=24,
    )


def feed_weight_grad(clock, exchanged, weight, gain):
    own, columns = weight.shape
    shards, ff, _ = exchanged.shape
    join = 128 // math.gcd(ff, 128)

    def body(ins, w, g, grad_out, sum_out):
        value = ins[...].reshape(join * ff, own).astype(F32).T * g[...]
        grad_out[...] = value

        @pl.when(pl.program_id(0) == 0)
        def _():
            sum_out[...] = jnp.zeros_like(sum_out)

        total = jnp.sum(w[...].astype(F32) * value, -1, keepdims=True)
        sum_out[...] += jnp.broadcast_to(total, sum_out.shape)

    spec = pl.BlockSpec((join, ff, own), lambda i: (i, 0, 0))
    total = shape_of(own, 128, F32)
    return clock.call(
        body, [exchanged, weight, gain], [spec, column_blocks(own, join * ff), whole(gain)],
        [shape_of(own, columns, F32), total], [column_blocks(own, join * ff), whole_out(total)], shards // join,
    )


def qkv_weight_grad(clock, part, wq, wk, wv, gain):
    shards, cols, own = part.shape
    qcols, kv = wq.shape[1] // shards, wk.shape[1]
    sharing = shards * HEAD_SIZE // kv

    def body(ins, wq, wk, wv, g, q_out, k_out, v_out, sum_out):
        total = jnp.zeros((own, 1), F32)
        tails = []
        for j in range(shards):
            value = ins[j].astype(F32).T * g[...]
            at = pl.ds(j * qcols, qcols)
            q_out[:, at] = value[:, :qcols]
            total += jnp.sum(wq[:, at].astype(F32) * value[:, :qcols], -1, keepdims=True)
            tails.append(value[:, qcols:])
        tails = [sum(tails[j : j + sharing]) for j in range(0, shards, sharing)]
        for w, out, at in ((wk, k_out, 0), (wv, v_out, HEAD_SIZE)):
            value = jnp.concatenate([tail[:, at : at + HEAD_SIZE] for tail in tails], 1)
            out[...] = value
            total += jnp.sum(w[...].astype(F32) * value, -1, keepdims=True)
        sum_out[...] = jnp.broadcast_to(total, (own, 128))

    args = [part, wq, wk, wv, gain]
    outs = [shape_of(own, n, F32) for n in (shards * qcols, kv, kv, 128)]
    return clock.call(body, args, [whole(a) for a in args], outs, [whole_out(o) for o in outs])


def widen(clock, *parts):
    rows, width = sum(p.shape[0] for p in parts), parts[0].shape[1]

    def body(*refs):
        refs[-1][...] = jnp.concatenate([ref[...] for ref in refs[:-1]], 0).astype(F32)

    return clock.call(
        body, parts, [column_blocks(p.shape[0], width // 4) for p in parts],
        [shape_of(rows, width, F32)], [column_blocks(rows, width // 4)], 4,
    )[0]


def product(clock, lefts, rights, turned, block=512):
    rows = lefts[0].shape[0]
    width = rights[0].shape[0 if turned else 1]
    count = len(lefts)

    def body(*refs):
        pairs = zip(refs[:count], refs[count : 2 * count])
        multiply = dot_nt if turned else dot
        refs[-1][...] = sum(multiply(a[...], b[...]) for a, b in pairs).astype(BF16)

    return clock.call(
        body, [*lefts, *rights],
        [row_blocks(block, a.shape[1]) for a in lefts] + [whole(b) for b in rights],
        [shape_of(rows, width)], [row_blocks(block, width)], rows // block,
    )[0]


def weight_grad(clock, lefts, rights, parts, block=512):
    rows = lefts[0].shape[0] // parts
    width = rights[0].shape[1]
    count = len(lefts)

    def body(*refs):
        lefts, rights, outs = refs[:count], refs[count : 2 * count], refs[2 * count :]
        total = sum(dot(a[...], b[...]) for a, b in zip(lefts, rights)).astype(BF16)
        for at, out in enumerate(outs):
            out[...] = total[at * rows : (at + 1) * rows]

    return clock.call(
        body, [*lefts, *rights],
        [whole(a) for a in lefts] + [column_blocks(b.shape[0], block) for b in rights],
        [shape_of(rows, width)] * parts, [column_blocks(rows, block)] * parts, width // block,
    )


def on_device(shards, copies, tokens, gain1, wq, wk, wv, wo, gain2, wg, wu, wd, out_grad):
    seqs, length, width = tokens.shape
    rows = seqs * length
    clock = Clock()
    group, line = Group(shards, clock), Line(copies, clock)
    kv_heads = wk.shape[1] // HEAD_SIZE
    sharing = shards // kv_heads
    ff, qcols, own = wd.shape[0], wo.shape[0], wq.shape[0]
    cols = qcols + 2 * HEAD_SIZE
    g1 = gain1.astype(F32)[:, None]
    g2 = gain2.astype(F32)[:, None]
    flat = tokens.reshape(rows, width)
    low = out_grad.reshape(rows, width)

    x_steps = group.gather(flat)
    next(x_steps)

    def load_qkv(refs, j):
        wq, wk, wv, g = refs
        head = j // sharing * HEAD_SIZE
        parts = wq[:, j * qcols : (j + 1) * qcols], wk[:, head : head + HEAD_SIZE], wv[:, head : head + HEAD_SIZE]
        return (jnp.concatenate([p.astype(F32) for p in parts], 1) * g[...]).astype(BF16)

    qkv_steps = group.exchange(load_qkv, [wq, wk, wv, g1], own, cols)
    next(qkv_steps)
    next(x_steps)
    next(qkv_steps)

    share = own // copies

    def load_feed(refs, j):
        copy, wg, wu, g = refs
        at = pl.ds(pl.multiple_of(copy[0] * share, share), share)
        parts = [w[at, j * ff : (j + 1) * ff].astype(F32) * g[at, :] for w in (wg, wu)]
        return jnp.concatenate(parts, 0).astype(BF16)

    copy = jnp.asarray(line.me, jnp.int32).reshape(1)
    feed_steps = group.exchange(load_feed, [copy, wg, wu, g2], 2 * share, ff)
    next(feed_steps)
    drain(x_steps)
    x_all = group.gathered
    drain(qkv_steps)
    wqkv = group.exchanged.reshape(width, cols)
    next(feed_steps)

    attention = Attention(clock, length, qcols, wqkv, wo)
    qkv_o, inv_o, context_ot, part_o = attention.forward(x_all[1])
    other = group.partner(part_o)
    drain(feed_steps)
    share_steps = line.share(group.exchanged.reshape(shards, 2, share, ff))
    next(share_steps, None)
    group.ride(clock.tie(low))
    qkv_e, inv_e, context_et, part_e = attention.forward(x_all[0])
    h1_steps = group.scatter([(part_e, other)], low)
    next(h1_steps)
    next(share_steps, None)
    next(h1_steps)
    next(share_steps, None)
    drain(h1_steps)

    def first_half(at, total, x, h1, inv2, n2):
        value = x[at, :].astype(F32) + total
        inv = lax.rsqrt(jnp.mean(value * value, -1, keepdims=True) + EPS)
        h1[at, :] = value
        inv2[at, :] = jnp.broadcast_to(inv, (inv.shape[0], 128))
        n2[at, :] = (value * inv).astype(BF16)

    h1, inv2, n2 = group.finish_rows(
        first_half, group.terms[0], [flat], [shape_of(rows, width, F32), shape_of(rows, 128, F32), shape_of(rows, width)]
    )
    n2_steps = group.gather(n2)
    next(n2_steps)
    group.join_rider()
    dy = group.gathered
    next(n2_steps)
    drain(share_steps)
    wg_mine, wu_mine = assemble(clock, line.me, *line.shared)
    wg_mine, wu_mine = wg_mine.reshape(width, ff), wu_mine.reshape(width, ff)
    drain(n2_steps)
    n2 = group.gathered
    results = {}

    def sum_copies(name, parts):
        for at, part in enumerate(parts):
            line.queue(part, functools.partial(results.__setitem__, (name, at)))

    def exchange_back(*parts):
        def load(refs, j):
            blocks = [ref[:, j * own : (j + 1) * own] for ref in refs]
            return jnp.concatenate(blocks, 0) if len(blocks) > 1 else blocks[0]

        return group.exchange(load, parts, sum(part.shape[0] for part in parts), own)

    act_e, dgate_e, dup_e, act_et, dgate_et, dup_et = feed(clock, n2[0], dy[0], wg_mine, wu_mine, wd)
    act_o, dgate_o, dup_o, act_ot, dgate_ot, dup_ot = feed(clock, n2[1], dy[1], wg_mine, wu_mine, wd)
    sum_copies("down", weight_grad(clock, (act_et, act_ot), dy, 2))
    line.tick()
    other = group.partner(product(clock, (dgate_o, dup_o), (wg_mine, wu_mine), True))
    part_e = product(clock, (dgate_e, dup_e), (wg_mine, wu_mine), True)
    a2_steps = group.scatter([(part_e, other)])
    next(a2_steps)
    line.tick()
    sum_copies("gate", weight_grad(clock, (dgate_et, dgate_ot), n2, 2))
    sum_copies("up", weight_grad(clock, (dup_et, dup_ot), n2, 2))
    next(a2_steps)
    line.tick()
    drain(a2_steps)

    def second_half(at, total, dy, h1, inv2, dh1, low_out):
        value, inv = h1[at, :], inv2[at, :1]
        middle = jnp.mean(total * value, -1, keepdims=True)
        grad = dy[at, :].astype(F32) + inv * total - value * (inv * inv * inv) * middle
        dh1[at, :] = grad
        low_out[at, :] = grad.astype(BF16)

    dh1, dattn = group.finish_rows(
        second_half, group.terms[0], [low, h1, inv2], [shape_of(rows, width, F32), shape_of(rows, width)]
    )
    dattn_steps = group.gather(dattn)
    next(dattn_steps)
    out_parts = product(clock, (act_e,), (wd,), False), group.partner(product(clock, (act_o,), (wd,), False))
    next(dattn_steps)
    line.tick()
    drain(dattn_steps)
    dattn = group.gathered
    dqkv_et, part_e = attention.backward(dattn[0], qkv_e, inv_e)
    dqkv_ot, part_o = attention.backward(dattn[1], qkv_o, inv_o)
    other = group.partner(part_o)
    line.tick()
    a1_steps = group.scatter([(part_e, other), out_parts])
    next(a1_steps)
    sum_copies("qkv", weight_grad(clock, (dqkv_et, dqkv_ot), x_all, 1))
    sum_copies("o", weight_grad(clock, (context_et, context_ot), dattn, 1))
    line.tick()
    next(a1_steps)
    line.tick()
    drain(a1_steps)

    def output(at, total, h1, out):
        out[at, :] = (h1[at, :] + total).astype(BF16)

    def input_half(at, total, x, dh1, out):
        value = x[at, :].astype(F32)
        inv = lax.rsqrt(jnp.mean(value * value, -1, keepdims=True) + EPS)
        middle = jnp.mean(total * value, -1, keepdims=True)
        out[at, :] = dh1[at, :] + inv * total - value * (inv * inv * inv) * middle

    (input_grad,) = group.finish_rows(
        input_half, group.terms[0], [flat, dh1], [shape_of(rows, width, F32)]
    )
    (layer_out,) = group.finish_rows(output, group.terms[1], [h1], [shape_of(rows, width)])
    def tick_until(name, at):
        while (name, at) not in results:
            line.tick(4)

    tick_until("gate", 1)
    gate_steps = exchange_back(results["gate", 0], results["gate", 1])
    next(gate_steps)
    next(gate_steps)
    line.tick(4)
    down_grad = widen(clock, results["down", 0], results["down", 1])
    drain(gate_steps)
    gate_grad, gate_sums = feed_weight_grad(clock, group.exchanged, wg, g2)
    tick_until("up", 1)
    up_steps = exchange_back(results["up", 0], results["up", 1])
    next(up_steps)
    next(up_steps)
    tick_until("qkv", 0)
    qkv_steps = exchange_back(results["qkv", 0])
    next(qkv_steps)
    drain(up_steps)
    up_back = group.exchanged
    next(qkv_steps)
    up_grad, up_sums = feed_weight_grad(clock, up_back, wu, g2)
    tick_until("o", 0)
    o_grad = widen(clock, results["o", 0])
    drain(qkv_steps)
    q_grad, k_grad, v_grad, qkv_sums = qkv_weight_grad(clock, group.exchanged, wq, wk, wv, g1)

    gain1_grad = qkv_sums[:, 0] / g1[:, 0]
    gain2_grad = (gate_sums[:, 0] + up_sums[:, 0]) / g2[:, 0]
    return (
        layer_out.reshape(seqs, length, width),
        input_grad.reshape(seqs, length, width),
        gain1_grad,
        q_grad,
        k_grad,
        v_grad,
        o_grad,
        gain2_grad,
        gate_grad,
        up_grad,
        down_grad,
    )


def solution(mesh):
    rows = P(("shard", "rep"), None, None)
    vector, matrix = P("shard"), P("shard", None)
    return jax.shard_map(
        functools.partial(on_device, mesh.shape["shard"], mesh.shape["rep"]),
        mesh=mesh,
        in_specs=(rows, vector, matrix, matrix, matrix, matrix, vector, matrix, matrix, matrix, rows),
        out_specs=(rows, rows, vector, matrix, matrix, matrix, matrix, vector, matrix, matrix, matrix),
        check_vma=False,
    )
```

```python
import functools
import math

import jax
import jax.numpy as jnp
import numpy as np
from jax import lax
from jax.experimental import pallas as pl
from jax.experimental.pallas import tpu as pltpu
from jax.sharding import PartitionSpec as P

HEAD_SIZE = 64
EPS = 1e-05
F32 = jnp.float32
BF16 = jnp.bfloat16
ANY = pl.BlockSpec(memory_space=pl.ANY)
TOKEN = pl.BlockSpec(memory_space=pltpu.HBM)
PER_MIB = 1.4e10


def dot(left, right):
    return jnp.dot(left, right, preferred_element_type=F32)


def dot_nt(left, right):
    return lax.dot_general(left, right, (((1,), (1,)), ((), ())), preferred_element_type=F32)


def dot_tn(left, right):
    return lax.dot_general(left, right, (((0,), (0,)), ((), ())), preferred_element_type=F32)


def shape_of(rows, columns, dtype=BF16):
    return jax.ShapeDtypeStruct((rows, columns), dtype)


def row_blocks(rows, columns):
    return pl.BlockSpec((rows, columns), lambda i: (i, 0))


def row_block_at(rows, columns, at):
    return pl.BlockSpec((rows, columns), lambda i: (at, 0))


def column_blocks(rows, columns):
    return pl.BlockSpec((rows, columns), lambda i: (0, i))


def whole(array):
    zeros = (0,) * array.ndim
    return pl.BlockSpec(array.shape, lambda i: zeros, pipeline_mode=pl.Buffered(1))


def whole_out(array):
    zeros = (0,) * len(array.shape)
    return pl.BlockSpec(array.shape, lambda i: zeros)


class Clock:
    def __init__(self):
        self.token = jnp.zeros((8, 128), F32)

    def call(self, body, args, in_specs, outs, out_specs, steps=1, aliases=None, vmem=60, cost=1):
        n_in, n_out = len(args), len(outs)

        def kernel(*refs):
            body(*refs[:n_in], *refs[n_in + 1 : n_in + 1 + n_out])

        *results, self.token = pl.pallas_call(
            kernel,
            grid=(steps,),
            out_shape=(*outs, pltpu.HBM(self.token.shape, F32)),
            in_specs=[*in_specs, TOKEN],
            out_specs=(*out_specs, TOKEN),
            input_output_aliases={n_in: n_out, **(aliases or {})},
            compiler_params=pltpu.CompilerParams(vmem_limit_bytes=vmem << 20),
            cost_estimate=pl.CostEstimate(flops=cost, bytes_accessed=cost // 1000 + 1, transcendentals=0),
        )(*args, self.token)
        return results

    def pause(self, mib):
        self.call(nothing, [], [], [], [], vmem=1, cost=int(mib * PER_MIB))

    def tie(self, *values):
        outs = [jax.ShapeDtypeStruct(v.shape, v.dtype) for v in values]
        results = self.call(
            nothing, values, [ANY] * len(values), outs, [ANY] * len(values),
            aliases={i: i for i in range(len(values))}, vmem=1,
        )
        return results if len(results) > 1 else results[0]


def nothing(*refs):
    pass


class Line:
    def __init__(self, size, clock):
        self.size = size
        self.clock = clock
        self.me = lax.axis_index("rep")
        self.end = jnp.asarray((self.me == 0) | (self.me == size - 1), jnp.int32).reshape(1)
        self.waiting, self.coming, self.across, self.going = [], None, None, None

    def shift(self, value, pairs):
        return lax.ppermute(value, "rep", pairs)

    def queue(self, value, finish):
        if self.size == 4:
            self.waiting.append((value, finish))
        else:
            finish(lax.psum(value, "rep") if self.size > 1 else value)

    def busy(self):
        return bool(self.waiting or self.coming or self.across or self.going)

    def tick(self, mib=0.1):
        if not self.busy():
            return
        coming, across, going = self.coming, self.across, self.going
        fresh = self.waiting.pop(0) if self.waiting else None
        args, outs, jobs = [], [], []

        def use(*arrays):
            args.extend(arrays)
            return slice(len(args) - len(arrays), len(args))

        def give(array):
            outs.append(shape_of(*array.shape))
            return len(outs) - 1

        inward = [(0, 1), (3, 2)]
        outward = [(1, 0), (2, 3)]
        shared = across and fresh and across["value"].shape == fresh[0].shape
        if across:
            terms = [across["value"], across["arrived"]]
            if shared:
                jobs.append(("fresh", use(fresh[0], *terms), give(fresh[0])))
            else:
                jobs.append(("add", use(*terms), give(across["value"])))
        if coming:
            jobs.append(("add", use(coming["value"], coming["arrived"]), give(coming["value"])))

        if fresh and jobs and not shared:
            jobs.append(("pass", use(fresh[0]), give(fresh[0])))

        def body(end, *refs):
            ins, results = refs[: len(args)], refs[len(args) :]
            outer = end[0] > 0
            for kind, where, out in jobs:
                mine = [ref[...].astype(F32) for ref in ins[where]]
                if kind == "pass":
                    value = mine[0]
                elif kind == "add":
                    value = mine[0] + mine[1]
                else:
                    value = jnp.where(outer, mine[0], mine[1] + mine[2])
                results[out][...] = value.astype(BF16)

        results = []
        if jobs:
            steps = 4
            specs = [column_blocks(a.shape[0], a.shape[1] // steps) for a in args]
            results = self.clock.call(
                body, [self.end, *args], [pl.BlockSpec(memory_space=pltpu.SMEM), *specs],
                outs, [column_blocks(o.shape[0], o.shape[1] // steps) for o in outs], steps, vmem=60,
            )
        results = list(results)
        self.going = self.across = self.coming = None
        if across:
            value = results.pop(0)
            arrived = self.shift(value, outward + (inward if shared else []))
            self.going = {"value": value, "arrived": arrived, "finish": across["finish"]}
        if coming:
            value = results.pop(0)
            self.across = {"value": value, "arrived": self.shift(value, [(1, 2), (2, 1)]), "finish": coming["finish"]}
        if fresh:
            value = fresh[0]
            if not shared:
                value = results.pop(0) if results else self.clock.tie(value)
                arrived = self.shift(value, inward)
            self.coming = {"value": value, "arrived": arrived, "finish": fresh[1]}
        self.clock.pause(mib)
        if going:
            going["finish"](self.select(going["arrived"], going["value"]))

    def select(self, ends, others):
        rows, width = others.shape

        def body(end, a, b, out):
            out[...] = jnp.where(end[0] > 0, a[...], b[...])

        spec = column_blocks(rows, width // 2)
        return self.clock.call(
            body, [self.end, ends, others], [pl.BlockSpec(memory_space=pltpu.SMEM), spec, spec],
            [shape_of(rows, width)], [spec], 2,
        )[0]


    def share(self, value):
        up, down = [value], [value]
        top = self.size - 1
        for step in range(top):
            pairs = [(i, i + 1) for i in range(step, top)]
            above = self.shift(up[-1], pairs)
            below = self.shift(down[-1], [(top - a, top - b) for a, b in pairs])
            self.clock.pause(0.1)
            yield
            above, below = self.clock.tie(above, below)
            up.append(above)
            down.append(below)
        self.shared = up, down


class Group:
    def __init__(self, size, clock):
        self.size = size
        self.clock = clock
        self.fast = size == 8
        self.me = jnp.asarray(lax.axis_index("shard"), jnp.int32).reshape(1)

    def swap(self, value, bit):
        return lax.ppermute(value, "shard", [(i, i ^ bit) for i in range(self.size)])

    def gather(self, own):
        half = own.shape[0] // 2
        if not self.fast:
            yield
            yield
            self.gather_all(own)
            return
        by_x, by_y = self.swap(own, 2), self.swap(own, 4)
        self.clock.pause(1)
        yield
        first, second = self.stacked([[[(by_x, 0)]], [[(by_y, 1)]]], half)
        first, second = self.swap(first, 4), self.swap(second, 2)
        self.clock.pause(0.6)
        yield
        self.join(own, [(by_x, 0), (by_x, 1), (by_y, 0), (by_y, 1), (first, 0), (second, 0)])

    def gather_all(self, own):
        every = lax.all_gather(own, "shard", axis=0, tiled=True)
        middle = every.shape[0] // 2
        self.gathered = every[:middle], every[middle:]

    def join(self, own, pieces):
        half, width = own.shape[0] // 2, own.shape[1]
        pieces = [(own, 0), (own, 1), *pieces]

        def body(*refs):
            for at, ref in enumerate(refs[:-1]):
                refs[-1][pl.ds(at * half, half), :] = ref[...]

        def columns(at):
            return pl.BlockSpec((half, width // 4), lambda i: (at, i))

        even = shape_of(half * self.size, width)
        even = self.clock.call(
            body, [array for array, _ in pieces], [columns(at) for _, at in pieces],
            [even], [column_blocks(even.shape[0], width // 4)], 4, vmem=24,
        )[0]
        self.gathered = even, self.swap(even, 1)
        self.clock.pause(4)

    def stacked(self, outs, rows):
        terms = [term for out in outs for block in out for term in block]
        width = terms[0][0].shape[1]

        def body(*refs):
            ins = iter(refs[: len(terms)])
            for out, ref in zip(outs, refs[len(terms) :]):
                for at, block in enumerate(out):
                    values = [next(ins)[...] for _ in block]
                    if len(values) > 1:
                        values = [sum(v.astype(F32) for v in values).astype(BF16)]
                    ref[pl.ds(at * rows, rows), :] = values[0]

        shapes = [shape_of(len(out) * rows, width) for out in outs]
        return self.clock.call(
            body, [array for array, _ in terms], [row_block_at(rows, width, at) for _, at in terms],
            shapes, [whole_out(o) for o in shapes], vmem=40,
        )

    def partner(self, odd):
        if not self.fast:
            return odd
        other = self.swap(odd, 1)
        self.clock.pause(4)
        return other

    def ride(self, own):
        if self.fast:
            self.riding = self.swap(own, 2), self.swap(own, 4)
            self.clock.pause(1)

    def scatter(self, sets, own=None):
        if not self.fast:
            yield
            yield
            both = [jnp.concatenate(pair, 0) for pair in sets]
            totals = [lax.psum_scatter(b, "shard", scatter_dimension=0, tiled=True) for b in both]
            self.terms = [[[(total, 0)], [(total, 1)]] for total in totals]
            if own is not None:
                self.gather_all(own)
            return
        rows = sets[0][0].shape[0] // 8
        rider = self.clock.tie(*self.riding) if own is not None else None

        def both(pair, at):
            return [(pair[0], at), (pair[1], at)]

        to_x = [both(pair, at) for pair in sets for at in (3, 7)]
        to_y = [both(pair, at) for pair in sets for at in (4, 6)]
        to_x, to_y = self.stacked([to_x, to_y], rows)
        by_x, by_y = self.swap(to_x, 2), self.swap(to_y, 4)
        self.clock.pause(len(sets))
        yield
        count = len(sets)
        to_x = [both(pair, 2) + [(by_y, 2 * i + 1)] for i, pair in enumerate(sets)]
        to_y = [both(pair, 5) + [(by_x, 2 * i + 1)] for i, pair in enumerate(sets)]
        if rider:
            to_x.append([(rider[1], 1)])
            to_y.append([(rider[0], 0)])
        to_x, to_y = self.stacked([to_x, to_y], rows)
        last_x, last_y = self.swap(to_x, 2), self.swap(to_y, 4)
        self.clock.pause(0.6 * len(sets) + 0.4 * bool(rider))
        yield
        self.terms = [
            [
                both(pair, 0) + [(by_y, 2 * i), (last_x, i)],
                both(pair, 1) + [(by_x, 2 * i), (last_y, i)],
            ]
            for i, pair in enumerate(sets)
        ]
        if rider:
            first = [(rider[0], 0), (rider[0], 1), (rider[1], 0), (rider[1], 1)]
            self.rider = own, [*first, (last_y, count), (last_x, count)]

    def join_rider(self):
        if self.fast:
            self.join(*self.rider)

    def finish_rows(self, body, terms, args, outs):
        flat = [array for half in terms for array, _ in half]
        rows = args[0].shape[0] // 2
        columns = flat[0].shape[1]
        specs = [row_block_at(rows, columns, at) for half in terms for _, at in half]
        count = len(terms[0])

        def kernel(*refs):
            sums, rest = refs[: len(flat)], refs[len(flat) :]
            for half in (0, 1):
                total = sum(ref[...].astype(F32) for ref in sums[half * count : (half + 1) * count])
                body(pl.ds(half * rows, rows), total, *rest)

        return self.clock.call(
            kernel, [*flat, *args], [*specs, *[whole(a) for a in args]], outs,
            [whole_out(o) for o in outs], vmem=40,
        )

    def exchange(self, load, args, a, b, apart=False):
        smem = pl.BlockSpec(memory_space=pltpu.SMEM)
        specs = [smem, *[smem if v.ndim == 1 else whole(v) for v in args]]
        if not self.fast:

            def lay(me, *refs):
                for j in range(self.size):
                    refs[-1][j] = load(refs[:-1], j)

            every = jax.ShapeDtypeStruct((self.size, a, b), BF16)
            blocks = self.clock.call(lay, [self.me, *args], specs, [every], [whole_out(every)])[0]
            yield
            yield
            self.exchanged = lax.all_to_all(blocks, "shard", split_axis=0, concat_axis=0)
            return
        four, two = jax.ShapeDtypeStruct((4, a, b), BF16), jax.ShapeDtypeStruct((2, a, b), BF16)

        def pack(me, *refs):
            kept, sent = refs[-2:]
            for j in range(8):
                value = load(refs[:-2], j)
                k = me[0] ^ j

                @pl.when(k & 1 == 0)
                def _(value=value, k=k):
                    kept[k >> 1] = value

                @pl.when(k & 1 == 1)
                def _(value=value, k=k):
                    sent[k >> 1] = value

        kept, sent = self.clock.call(
            pack, [self.me, *args], specs, [four] * 2, [whole_out(four)] * 2, vmem=32
        )
        come = self.swap(sent, 1)
        mib = 8 * a * b / 2**20
        self.clock.pause(mib)
        yield

        def stack(kept, come, *outs):
            for i, out in enumerate(outs):
                out[0] = kept[i + 1]
                out[1] = come[i + 1]

        sends = self.clock.call(
            stack, [kept, come], [whole(kept), whole(come)], [two] * 3, [whole_out(two)] * 3, vmem=24
        )
        arrived = [self.swap(value, 2 * i + 2) for i, value in enumerate(sends[: 2 if apart else 3])]
        self.clock.pause(mib / 2)
        yield
        if apart:
            arrived.append(self.swap(self.clock.tie(sends[2]), 6))
            self.clock.pause(mib / 2)
            yield

        def unpack(me, kept, come, *rest):
            out = rest[-1]
            out[me[0]] = kept[0]
            out[me[0] ^ 1] = come[0]
            for i, ref in enumerate(rest[:-1]):
                out[me[0] ^ (2 * i + 2)] = ref[0]
                out[me[0] ^ (2 * i + 3)] = ref[1]

        eight = jax.ShapeDtypeStruct((8, a, b), BF16)
        first = pl.BlockSpec((1, a, b), lambda i: (0, 0, 0))
        self.exchanged = self.clock.call(
            unpack, [self.me, kept, come, *arrived], [smem, first, first, *[whole(v) for v in arrived]],
            [eight], [whole_out(eight)], vmem=24,
        )[0]


def drain(steps):
    for _ in steps:
        pass


class Attention:
    def __init__(self, clock, length, qcols, wqkv, wo):
        self.clock, self.length, self.qcols = clock, length, qcols
        self.wqkv, self.wo = wqkv, wo
        self.heads = qcols // HEAD_SIZE
        self.width = qcols + 2 * HEAD_SIZE
        half = HEAD_SIZE // 2
        freqs = 1.0 / 10000.0 ** (np.arange(half, dtype=np.float32) * 2.0 / HEAD_SIZE)
        angles = np.arange(length, dtype=np.float32)[:, None] * freqs[None, :].astype(np.float32)
        turns = self.heads + 1
        low = np.arange(turns * HEAD_SIZE) % HEAD_SIZE < half
        cosine = np.tile(np.cos(angles), (1, 2 * turns))
        sine = np.tile(np.sin(angles), (1, 2 * turns))
        plain = np.zeros((length, HEAD_SIZE), np.float32)
        self.tables = tuple(
            jnp.asarray(np.concatenate(pair, 1), F32)
            for pair in (
                (cosine, plain + 1.0),
                (np.where(low, -sine, 0.0), plain),
                (np.where(low, 0.0, sine), plain),
            )
        )

    def roll(self, value, by):
        return pltpu.roll(value, by % value.shape[1], 1)

    def stack(self, value):
        head = lax.broadcasted_iota(jnp.int32, value.shape, 1) // HEAD_SIZE
        return jnp.concatenate([jnp.where(head == h, value, 0.0) for h in range(self.heads)], 0).astype(BF16)

    def unstack(self, value):
        head = lax.broadcasted_iota(jnp.int32, (self.length, self.qcols), 1) // HEAD_SIZE
        total = jnp.zeros((self.length, self.qcols), F32)
        for h in range(self.heads):
            total = jnp.where(head == h, value[h * self.length : (h + 1) * self.length], total)
        return total

    def repeated(self, value):
        first = lax.broadcasted_iota(jnp.int32, value.shape, 1) < HEAD_SIZE
        turned = self.roll(value, HEAD_SIZE)
        times = self.qcols // (2 * HEAD_SIZE)
        key = jnp.where(first, value, turned).astype(BF16)
        val = jnp.where(first, turned, value).astype(BF16)
        return jnp.concatenate([key] * times, 1), jnp.concatenate([val] * times, 1)

    def probabilities(self, stacked, keys):
        raw = dot_nt(stacked, keys) * (1.0 / math.sqrt(HEAD_SIZE))
        raw = raw.reshape(self.heads, self.length, self.length)
        at = lax.broadcasted_iota(jnp.int32, raw.shape, 1)
        seen = lax.broadcasted_iota(jnp.int32, raw.shape, 2) <= at
        scores = jnp.where(seen, raw, -1e30)
        e = jnp.exp(scores - jnp.max(scores, -1, keepdims=True))
        prob = e / jnp.sum(e, -1, keepdims=True)
        return prob.reshape(self.heads * self.length, self.length)

    def forward(self, tokens):
        rows, width = tokens.shape
        block, length, qcols = 2 * self.length, self.length, self.qcols

        def body(x, wqkv, wo, c, s1, s2, qkv_out, inv_out, context_t, partial_out):
            source = x[...].astype(F32)
            inv = lax.rsqrt(jnp.mean(source * source, -1, keepdims=True) + EPS)
            inv_out[...] = jnp.broadcast_to(inv, (block, 128))
            lin = dot(x[...], wqkv[...]) * inv
            contexts = []
            for at in range(0, block, length):
                v = lin[at : at + length]
                v = v * c[...] + self.roll(v, -32) * s1[...] + self.roll(v, 32) * s2[...]
                v = v.astype(BF16).astype(F32)
                qkv_out[pl.ds(at, length), :] = v.astype(BF16)
                keys, values = self.repeated(v[:, qcols:])
                prob = self.probabilities(self.stack(v[:, :qcols]), keys)
                context = self.unstack(dot(prob.astype(BF16), values))
                contexts.append(context.astype(BF16))
            context = jnp.concatenate(contexts, 0)
            context_t[...] = context.T
            partial_out[...] = dot(context, wo[...]).astype(BF16)

        args = (tokens, self.wqkv, self.wo, *self.tables)
        return self.clock.call(
            body, args, [row_blocks(block, width), *[whole(a) for a in args[1:]]],
            [shape_of(rows, self.width), shape_of(rows, 128, F32), shape_of(qcols, rows), shape_of(rows, width)],
            [
                row_blocks(block, self.width),
                row_blocks(block, 128),
                column_blocks(qcols, block),
                row_blocks(block, width),
            ],
            rows // block,
        )

    def backward(self, grad, qkv, inv):
        rows, width = grad.shape
        block, length, qcols = 2 * self.length, self.length, self.qcols
        scale = 1.0 / math.sqrt(HEAD_SIZE)

        def fold(value):
            folded = sum(value[:, i : i + 2 * HEAD_SIZE] for i in range(0, qcols, 2 * HEAD_SIZE))
            return folded + self.roll(folded, HEAD_SIZE)

        def body(d, qkv_in, inv_in, wqkv, wo, c, s1, s2, grad_t, partial_out):
            grads = []
            dcontext = dot_nt(d[...], wo[...]).astype(BF16).astype(F32)
            for at in range(0, block, length):
                v = qkv_in[pl.ds(at, length), :].astype(F32)
                keys, values = self.repeated(v[:, qcols:])
                stacked = self.stack(v[:, :qcols])
                prob = self.probabilities(stacked, keys)
                dstacked = self.stack(dcontext[at : at + length])
                dprob = dot_nt(dstacked, values)
                dvalue = fold(dot_tn(prob.astype(BF16), dstacked))
                ds = prob * (dprob - jnp.sum(prob * dprob, -1, keepdims=True))
                ds = ds.astype(BF16)
                dq = self.unstack(dot(ds, keys)) * scale
                dkey = fold(dot_tn(ds, stacked)) * scale
                first = lax.broadcasted_iota(jnp.int32, dkey.shape, 1) < HEAD_SIZE
                g = jnp.concatenate([dq, jnp.where(first, dkey, dvalue)], 1)
                g = g * c[...] - self.roll(g, -32) * s1[...] - self.roll(g, 32) * s2[...]
                grads.append(g)
            g = jnp.concatenate(grads, 0)
            grad_t[...] = (g * inv_in[:, :1]).astype(BF16).T
            partial_out[...] = dot_nt(g.astype(BF16), wqkv[...]).astype(BF16)

        args = (grad, qkv, inv, self.wqkv, self.wo, *self.tables)
        return self.clock.call(
            body, args,
            [
                row_blocks(block, width),
                row_blocks(block, self.width),
                row_blocks(block, 128),
                *[whole(a) for a in args[3:]],
            ],
            [shape_of(self.width, rows), shape_of(rows, width)],
            [column_blocks(self.width, block), row_blocks(block, width)],
            rows // block,
        )


def feed(clock, normed, dy, wg, wu, wd, block=256):
    rows, width = normed.shape
    ff = wd.shape[0]

    def body(x, d, wg, wu, wd, act_out, dgate_out, dup_out, act_t, dgate_t, dup_t):
        gate = dot(x[...], wg[...])
        up = dot(x[...], wu[...])
        dact = dot_nt(d[...], wd[...])
        sigma = jax.nn.sigmoid(gate)
        silu = gate * sigma
        act = (silu * up).astype(BF16)
        dgate = (dact * up * (sigma * (1.0 + gate * (1.0 - sigma)))).astype(BF16)
        dup = (dact * silu).astype(BF16)
        for value, out, turned in ((act, act_out, act_t), (dgate, dgate_out, dgate_t), (dup, dup_out, dup_t)):
            out[...] = value
            turned[...] = value.T

    args = (normed, dy, wg, wu, wd)
    return clock.call(
        body, args, [row_blocks(block, width)] * 2 + [whole(a) for a in args[2:]],
        [shape_of(rows, ff)] * 3 + [shape_of(ff, rows)] * 3,
        [row_blocks(block, ff)] * 3 + [column_blocks(ff, block)] * 3,
        rows // block,
    )


def assemble(clock, me, above, below):
    copies = len(above)
    a, _, b, c = above[0].shape

    def body(me_ref, *refs):
        outs = refs[2 * copies - 1 :]
        for step in range(copies):
            at = lax.rem(me_ref[0] + step, copies)

            def store(ref, at=at):
                for which, out in enumerate(outs):
                    out[0, at] = ref[0, which]

            if step == 0:
                store(refs[0])
                continue

            @pl.when(me_ref[0] + step < copies)
            def _(ref=refs[copies + step - 1], store=store):
                store(ref)

            @pl.when(me_ref[0] + step >= copies)
            def _(ref=refs[copies - step], store=store):
                store(ref)

    args = [*above, *below[1:]]
    out = jax.ShapeDtypeStruct((a, copies, b, c), BF16)
    spec = pl.BlockSpec((1, 2, b, c), lambda i: (i, 0, 0, 0))
    out_spec = pl.BlockSpec((1, copies, b, c), lambda i: (i, 0, 0, 0))
    me = jnp.asarray(me, jnp.int32).reshape(1)
    return clock.call(
        body, [me, *args], [pl.BlockSpec(memory_space=pltpu.SMEM)] + [spec] * len(args),
        [out] * 2, [out_spec] * 2, a, vmem=24,
    )


def feed_weight_grad(clock, exchanged, weight, gain):
    own, columns = weight.shape
    shards, ff, _ = exchanged.shape
    join = 128 // math.gcd(ff, 128)

    def body(ins, w, g, grad_out, sum_out):
        value = ins[...].reshape(join * ff, own).astype(F32).T * g[...]
        grad_out[...] = value

        @pl.when(pl.program_id(0) == 0)
        def _():
            sum_out[...] = jnp.zeros_like(sum_out)

        total = jnp.sum(w[...].astype(F32) * value, -1, keepdims=True)
        sum_out[...] += jnp.broadcast_to(total, sum_out.shape)

    spec = pl.BlockSpec((join, ff, own), lambda i: (i, 0, 0))
    total = shape_of(own, 128, F32)
    return clock.call(
        body, [exchanged, weight, gain], [spec, column_blocks(own, join * ff), whole(gain)],
        [shape_of(own, columns, F32), total], [column_blocks(own, join * ff), whole_out(total)], shards // join,
    )


def qkv_weight_grad(clock, part, wq, wk, wv, gain):
    shards, cols, own = part.shape
    qcols, kv = wq.shape[1] // shards, wk.shape[1]
    sharing = shards * HEAD_SIZE // kv

    def body(ins, wq, wk, wv, g, q_out, k_out, v_out, sum_out):
        total = jnp.zeros((own, 1), F32)
        tails = []
        for j in range(shards):
            value = ins[j].astype(F32).T * g[...]
            at = pl.ds(j * qcols, qcols)
            q_out[:, at] = value[:, :qcols]
            total += jnp.sum(wq[:, at].astype(F32) * value[:, :qcols], -1, keepdims=True)
            tails.append(value[:, qcols:])
        tails = [sum(tails[j : j + sharing]) for j in range(0, shards, sharing)]
        for w, out, at in ((wk, k_out, 0), (wv, v_out, HEAD_SIZE)):
            value = jnp.concatenate([tail[:, at : at + HEAD_SIZE] for tail in tails], 1)
            out[...] = value
            total += jnp.sum(w[...].astype(F32) * value, -1, keepdims=True)
        sum_out[...] = jnp.broadcast_to(total, (own, 128))

    args = [part, wq, wk, wv, gain]
    outs = [shape_of(own, n, F32) for n in (shards * qcols, kv, kv, 128)]
    return clock.call(body, args, [whole(a) for a in args], outs, [whole_out(o) for o in outs])


def widen(clock, *parts):
    rows, width = sum(p.shape[0] for p in parts), parts[0].shape[1]

    def body(*refs):
        refs[-1][...] = jnp.concatenate([ref[...] for ref in refs[:-1]], 0).astype(F32)

    return clock.call(
        body, parts, [column_blocks(p.shape[0], width // 4) for p in parts],
        [shape_of(rows, width, F32)], [column_blocks(rows, width // 4)], 4,
    )[0]


def product(clock, lefts, rights, turned, block=512):
    rows = lefts[0].shape[0]
    width = rights[0].shape[0 if turned else 1]
    count = len(lefts)

    def body(*refs):
        pairs = zip(refs[:count], refs[count : 2 * count])
        multiply = dot_nt if turned else dot
        refs[-1][...] = sum(multiply(a[...], b[...]) for a, b in pairs).astype(BF16)

    return clock.call(
        body, [*lefts, *rights],
        [row_blocks(block, a.shape[1]) for a in lefts] + [whole(b) for b in rights],
        [shape_of(rows, width)], [row_blocks(block, width)], rows // block,
    )[0]


def weight_grad(clock, lefts, rights, parts, block=512, part=None):
    rows = lefts[0].shape[0] // parts
    if part is not None:
        parts = 1
    at = part or 0
    width = rights[0].shape[1]
    count = len(lefts)

    def body(*refs):
        lefts, rights, outs = refs[:count], refs[count : 2 * count], refs[2 * count :]
        total = sum(dot(a[...], b[...]) for a, b in zip(lefts, rights)).astype(BF16)
        for i, out in enumerate(outs):
            out[...] = total[i * rows : (i + 1) * rows]

    def left(array):
        return pl.BlockSpec((rows * parts, array.shape[1]), lambda i: (at, 0), pipeline_mode=pl.Buffered(1))

    return clock.call(
        body, [*lefts, *rights],
        [left(a) for a in lefts] + [column_blocks(b.shape[0], block) for b in rights],
        [shape_of(rows, width)] * parts, [column_blocks(rows, block)] * parts, width // block,
    )


def on_device(shards, copies, tokens, gain1, wq, wk, wv, wo, gain2, wg, wu, wd, out_grad):
    seqs, length, width = tokens.shape
    rows = seqs * length
    clock = Clock()
    group, line = Group(shards, clock), Line(copies, clock)
    kv_heads = wk.shape[1] // HEAD_SIZE
    sharing = shards // kv_heads
    ff, qcols, own = wd.shape[0], wo.shape[0], wq.shape[0]
    cols = qcols + 2 * HEAD_SIZE
    g1 = gain1.astype(F32)[:, None]
    g2 = gain2.astype(F32)[:, None]
    flat = tokens.reshape(rows, width)
    low = out_grad.reshape(rows, width)

    x_steps = group.gather(flat)
    next(x_steps)

    def load_qkv(refs, j):
        wq, wk, wv, g = refs
        head = j // sharing * HEAD_SIZE
        parts = wq[:, j * qcols : (j + 1) * qcols], wk[:, head : head + HEAD_SIZE], wv[:, head : head + HEAD_SIZE]
        return (jnp.concatenate([p.astype(F32) for p in parts], 1) * g[...]).astype(BF16)

    qkv_steps = group.exchange(load_qkv, [wq, wk, wv, g1], own, cols)
    next(qkv_steps)
    next(x_steps)
    next(qkv_steps)

    share = own // copies

    def load_feed(refs, j):
        copy, wg, wu, g = refs
        at = pl.ds(pl.multiple_of(copy[0] * share, share), share)
        parts = [w[at, j * ff : (j + 1) * ff].astype(F32) * g[at, :] for w in (wg, wu)]
        return jnp.concatenate(parts, 0).astype(BF16)

    copy = jnp.asarray(line.me, jnp.int32).reshape(1)
    feed_steps = group.exchange(load_feed, [copy, wg, wu, g2], 2 * share, ff)
    next(feed_steps)
    drain(x_steps)
    x_all = group.gathered
    drain(qkv_steps)
    wqkv = group.exchanged.reshape(width, cols)
    next(feed_steps)

    attention = Attention(clock, length, qcols, wqkv, wo)
    qkv_o, inv_o, context_ot, part_o = attention.forward(x_all[1])
    other = group.partner(part_o)
    drain(feed_steps)
    share_steps = line.share(group.exchanged.reshape(shards, 2, share, ff))
    next(share_steps, None)
    group.ride(clock.tie(low))
    qkv_e, inv_e, context_et, part_e = attention.forward(x_all[0])
    h1_steps = group.scatter([(part_e, other)], low)
    next(h1_steps)
    next(share_steps, None)
    next(h1_steps)
    next(share_steps, None)
    drain(h1_steps)

    def first_half(at, total, x, h1, inv2, n2):
        value = x[at, :].astype(F32) + total
        inv = lax.rsqrt(jnp.mean(value * value, -1, keepdims=True) + EPS)
        h1[at, :] = value
        inv2[at, :] = jnp.broadcast_to(inv, (inv.shape[0], 128))
        n2[at, :] = (value * inv).astype(BF16)

    h1, inv2, n2 = group.finish_rows(
        first_half, group.terms[0], [flat], [shape_of(rows, width, F32), shape_of(rows, 128, F32), shape_of(rows, width)]
    )
    n2_steps = group.gather(n2)
    next(n2_steps)
    group.join_rider()
    dy = group.gathered
    next(n2_steps)
    drain(share_steps)
    wg_mine, wu_mine = assemble(clock, line.me, *line.shared)
    wg_mine, wu_mine = wg_mine.reshape(width, ff), wu_mine.reshape(width, ff)
    drain(n2_steps)
    n2 = group.gathered
    results = {}

    def sum_copies(name, parts):
        for at, part in enumerate(parts):
            line.queue(part, functools.partial(results.__setitem__, (name, at)))

    def exchange_back(*parts, apart=False):
        def load(refs, j):
            blocks = [ref[:, j * own : (j + 1) * own] for ref in refs]
            return jnp.concatenate(blocks, 0) if len(blocks) > 1 else blocks[0]

        return group.exchange(load, parts, sum(part.shape[0] for part in parts), own, apart)

    act_e, dgate_e, dup_e, act_et, dgate_et, dup_et = feed(clock, n2[0], dy[0], wg_mine, wu_mine, wd)
    act_o, dgate_o, dup_o, act_ot, dgate_ot, dup_ot = feed(clock, n2[1], dy[1], wg_mine, wu_mine, wd)
    first = weight_grad(clock, (act_et, act_ot), dy, 2, part=0)
    line.queue(first[0], functools.partial(results.__setitem__, ("down", 0)))
    line.tick()
    second = weight_grad(clock, (act_et, act_ot), dy, 2, part=1)
    line.queue(second[0], functools.partial(results.__setitem__, ("down", 1)))
    other = group.partner(product(clock, (dgate_o, dup_o), (wg_mine, wu_mine), True))
    part_e = product(clock, (dgate_e, dup_e), (wg_mine, wu_mine), True)
    a2_steps = group.scatter([(part_e, other)])
    next(a2_steps)
    line.tick()
    sum_copies("gate", weight_grad(clock, (dgate_et, dgate_ot), n2, 2))
    sum_copies("up", weight_grad(clock, (dup_et, dup_ot), n2, 2))
    next(a2_steps)
    line.tick()
    drain(a2_steps)

    def second_half(at, total, dy, h1, inv2, dh1, low_out):
        value, inv = h1[at, :], inv2[at, :1]
        middle = jnp.mean(total * value, -1, keepdims=True)
        grad = dy[at, :].astype(F32) + inv * total - value * (inv * inv * inv) * middle
        dh1[at, :] = grad
        low_out[at, :] = grad.astype(BF16)

    dh1, dattn = group.finish_rows(
        second_half, group.terms[0], [low, h1, inv2], [shape_of(rows, width, F32), shape_of(rows, width)]
    )
    dattn_steps = group.gather(dattn)
    next(dattn_steps)
    out_parts = product(clock, (act_e,), (wd,), False), group.partner(product(clock, (act_o,), (wd,), False))
    next(dattn_steps)
    line.tick()
    drain(dattn_steps)
    dattn = group.gathered
    dqkv_et, part_e = attention.backward(dattn[0], qkv_e, inv_e)
    dqkv_ot, part_o = attention.backward(dattn[1], qkv_o, inv_o)
    other = group.partner(part_o)
    line.tick()
    a1_steps = group.scatter([(part_e, other), out_parts])
    next(a1_steps)
    sum_copies("qkv", weight_grad(clock, (dqkv_et, dqkv_ot), x_all, 1))
    sum_copies("o", weight_grad(clock, (context_et, context_ot), dattn, 1))
    line.tick()
    next(a1_steps)
    line.tick()
    drain(a1_steps)

    def output(at, total, h1, out):
        out[at, :] = (h1[at, :] + total).astype(BF16)

    def input_half(at, total, x, dh1, out):
        value = x[at, :].astype(F32)
        inv = lax.rsqrt(jnp.mean(value * value, -1, keepdims=True) + EPS)
        middle = jnp.mean(total * value, -1, keepdims=True)
        out[at, :] = dh1[at, :] + inv * total - value * (inv * inv * inv) * middle

    (input_grad,) = group.finish_rows(
        input_half, group.terms[0], [flat, dh1], [shape_of(rows, width, F32)]
    )
    (layer_out,) = group.finish_rows(output, group.terms[1], [h1], [shape_of(rows, width)])
    def tick_until(name, at):
        while (name, at) not in results:
            line.tick(0.1)

    tick_until("gate", 1)
    gate_steps = exchange_back(results["gate", 0], results["gate", 1], apart=True)
    next(gate_steps)
    line.tick(4)
    next(gate_steps)
    down_grad = widen(clock, results["down", 0], results["down", 1])
    tick_until("up", 1)
    next(gate_steps, None)
    up_steps = exchange_back(results["up", 0], results["up", 1])
    next(up_steps)
    drain(gate_steps)
    gate_grad, gate_sums = feed_weight_grad(clock, group.exchanged, wg, g2)
    next(up_steps)
    tick_until("qkv", 0)
    qkv_steps = exchange_back(results["qkv", 0])
    next(qkv_steps)
    drain(up_steps)
    up_back = group.exchanged
    next(qkv_steps)
    up_grad, up_sums = feed_weight_grad(clock, up_back, wu, g2)
    tick_until("o", 0)
    o_grad = widen(clock, results["o", 0])
    drain(qkv_steps)
    q_grad, k_grad, v_grad, qkv_sums = qkv_weight_grad(clock, group.exchanged, wq, wk, wv, g1)

    gain1_grad = qkv_sums[:, 0] / g1[:, 0]
    gain2_grad = (gate_sums[:, 0] + up_sums[:, 0]) / g2[:, 0]
    return (
        layer_out.reshape(seqs, length, width),
        input_grad.reshape(seqs, length, width),
        gain1_grad,
        q_grad,
        k_grad,
        v_grad,
        o_grad,
        gain2_grad,
        gate_grad,
        up_grad,
        down_grad,
    )


def solution(mesh):
    rows = P(("shard", "rep"), None, None)
    vector, matrix = P("shard"), P("shard", None)
    return jax.shard_map(
        functools.partial(on_device, mesh.shape["shard"], mesh.shape["rep"]),
        mesh=mesh,
        in_specs=(rows, vector, matrix, matrix, matrix, matrix, vector, matrix, matrix, matrix, rows),
        out_specs=(rows, rows, vector, matrix, matrix, matrix, matrix, vector, matrix, matrix, matrix),
        check_vma=False,
    )
```

```python
import functools
import math

import jax
import jax.numpy as jnp
import numpy as np
from jax import lax
from jax.experimental import pallas as pl
from jax.experimental.pallas import tpu as pltpu
from jax.sharding import PartitionSpec as P

HEAD_SIZE = 64
EPS = 1e-05
F32 = jnp.float32
BF16 = jnp.bfloat16
ANY = pl.BlockSpec(memory_space=pl.ANY)
TOKEN = pl.BlockSpec(memory_space=pltpu.HBM)
PER_MIB = 1.4e10


def dot(left, right):
    return jnp.dot(left, right, preferred_element_type=F32)


def dot_nt(left, right):
    return lax.dot_general(left, right, (((1,), (1,)), ((), ())), preferred_element_type=F32)


def dot_tn(left, right):
    return lax.dot_general(left, right, (((0,), (0,)), ((), ())), preferred_element_type=F32)


def shape_of(rows, columns, dtype=BF16):
    return jax.ShapeDtypeStruct((rows, columns), dtype)


def row_blocks(rows, columns):
    return pl.BlockSpec((rows, columns), lambda i: (i, 0))


def row_block_at(rows, columns, at):
    return pl.BlockSpec((rows, columns), lambda i: (at, 0))


def column_blocks(rows, columns):
    return pl.BlockSpec((rows, columns), lambda i: (0, i))


def whole(array):
    zeros = (0,) * array.ndim
    return pl.BlockSpec(array.shape, lambda i: zeros, pipeline_mode=pl.Buffered(1))


def whole_out(array):
    zeros = (0,) * len(array.shape)
    return pl.BlockSpec(array.shape, lambda i: zeros)


class Clock:
    def __init__(self):
        self.token = jnp.zeros((8, 128), F32)

    def call(self, body, args, in_specs, outs, out_specs, steps=1, aliases=None, vmem=60, cost=1):
        n_in, n_out = len(args), len(outs)

        def kernel(*refs):
            body(*refs[:n_in], *refs[n_in + 1 : n_in + 1 + n_out])

        *results, self.token = pl.pallas_call(
            kernel,
            grid=(steps,),
            out_shape=(*outs, pltpu.HBM(self.token.shape, F32)),
            in_specs=[*in_specs, TOKEN],
            out_specs=(*out_specs, TOKEN),
            input_output_aliases={n_in: n_out, **(aliases or {})},
            compiler_params=pltpu.CompilerParams(vmem_limit_bytes=vmem << 20),
            cost_estimate=pl.CostEstimate(flops=cost, bytes_accessed=cost // 1000 + 1, transcendentals=0),
        )(*args, self.token)
        return results

    def pause(self, mib):
        self.call(nothing, [], [], [], [], vmem=1, cost=int(mib * PER_MIB))

    def tie(self, *values):
        outs = [jax.ShapeDtypeStruct(v.shape, v.dtype) for v in values]
        results = self.call(
            nothing, values, [ANY] * len(values), outs, [ANY] * len(values),
            aliases={i: i for i in range(len(values))}, vmem=1,
        )
        return results if len(results) > 1 else results[0]


def nothing(*refs):
    pass


class Line:
    def __init__(self, size, clock):
        self.size = size
        self.clock = clock
        self.me = lax.axis_index("rep")
        self.end = jnp.asarray((self.me == 0) | (self.me == size - 1), jnp.int32).reshape(1)
        self.waiting, self.coming, self.across, self.going = [], None, None, None

    def shift(self, value, pairs):
        return lax.ppermute(value, "rep", pairs)

    def queue(self, value, finish):
        if self.size == 4:
            self.waiting.append((value, finish))
        else:
            finish(lax.psum(value, "rep") if self.size > 1 else value)

    def busy(self):
        return bool(self.waiting or self.coming or self.across or self.going)

    def tick(self, mib=0.1):
        if not self.busy():
            return
        coming, across, going = self.coming, self.across, self.going
        fresh = self.waiting.pop(0) if self.waiting else None
        args, outs, jobs = [], [], []

        def use(*arrays):
            args.extend(arrays)
            return slice(len(args) - len(arrays), len(args))

        def give(array):
            outs.append(shape_of(*array.shape))
            return len(outs) - 1

        inward = [(0, 1), (3, 2)]
        outward = [(1, 0), (2, 3)]
        shared = across and fresh and across["value"].shape == fresh[0].shape
        if across:
            terms = [across["value"], across["arrived"]]
            if shared:
                jobs.append(("fresh", use(fresh[0], *terms), give(fresh[0])))
            else:
                jobs.append(("add", use(*terms), give(across["value"])))
        if coming:
            jobs.append(("add", use(coming["value"], coming["arrived"]), give(coming["value"])))

        if fresh and jobs and not shared:
            jobs.append(("pass", use(fresh[0]), give(fresh[0])))

        def body(end, *refs):
            ins, results = refs[: len(args)], refs[len(args) :]
            outer = end[0] > 0
            for kind, where, out in jobs:
                mine = [ref[...].astype(F32) for ref in ins[where]]
                if kind == "pass":
                    value = mine[0]
                elif kind == "add":
                    value = mine[0] + mine[1]
                else:
                    value = jnp.where(outer, mine[0], mine[1] + mine[2])
                results[out][...] = value.astype(BF16)

        results = []
        if jobs:
            steps = 2 if all(a.shape[0] % 32 == 0 for a in args) else 1
            specs = [row_blocks(a.shape[0] // steps, a.shape[1]) for a in args]
            results = self.clock.call(
                body, [self.end, *args], [pl.BlockSpec(memory_space=pltpu.SMEM), *specs],
                outs, [row_blocks(o.shape[0] // steps, o.shape[1]) for o in outs], steps, vmem=60,
            )
        results = list(results)
        self.going = self.across = self.coming = None
        if across:
            value = results.pop(0)
            arrived = self.shift(value, outward + (inward if shared else []))
            self.going = {"value": value, "arrived": arrived, "finish": across["finish"]}
        if coming:
            value = results.pop(0)
            self.across = {"value": value, "arrived": self.shift(value, [(1, 2), (2, 1)]), "finish": coming["finish"]}
        if fresh:
            value = fresh[0]
            if not shared:
                value = results.pop(0) if results else self.clock.tie(value)
                arrived = self.shift(value, inward)
            self.coming = {"value": value, "arrived": arrived, "finish": fresh[1]}
        self.clock.pause(mib)
        if going:
            going["finish"](self.select(going["arrived"], going["value"]))

    def select(self, ends, others):
        rows, width = others.shape

        def body(end, a, b, out):
            out[...] = jnp.where(end[0] > 0, a[...], b[...])

        spec = column_blocks(rows, width // 2)
        return self.clock.call(
            body, [self.end, ends, others], [pl.BlockSpec(memory_space=pltpu.SMEM), spec, spec],
            [shape_of(rows, width)], [spec], 2,
        )[0]


    def share(self, value):
        up, down = [value], [value]
        top = self.size - 1
        for step in range(top):
            pairs = [(i, i + 1) for i in range(step, top)]
            above = self.shift(up[-1], pairs)
            below = self.shift(down[-1], [(top - a, top - b) for a, b in pairs])
            self.clock.pause(0.1)
            yield
            above, below = self.clock.tie(above, below)
            up.append(above)
            down.append(below)
        self.shared = up, down


class Group:
    def __init__(self, size, clock):
        self.size = size
        self.clock = clock
        self.fast = size == 8
        self.me = jnp.asarray(lax.axis_index("shard"), jnp.int32).reshape(1)

    def swap(self, value, bit):
        return lax.ppermute(value, "shard", [(i, i ^ bit) for i in range(self.size)])

    def gather(self, own):
        half = own.shape[0] // 2
        if not self.fast:
            yield
            yield
            self.gather_all(own)
            return
        by_x, by_y = self.swap(own, 2), self.swap(own, 4)
        self.clock.pause(1)
        yield
        first, second = self.stacked([[[(by_x, 0)]], [[(by_y, 1)]]], half)
        first, second = self.swap(first, 4), self.swap(second, 2)
        self.clock.pause(0.6)
        yield
        self.join(own, [(by_x, 0), (by_x, 1), (by_y, 0), (by_y, 1), (first, 0), (second, 0)])

    def gather_all(self, own):
        every = lax.all_gather(own, "shard", axis=0, tiled=True)
        middle = every.shape[0] // 2
        self.gathered = every[:middle], every[middle:]

    def join(self, own, pieces):
        half, width = own.shape[0] // 2, own.shape[1]
        pieces = [(own, 0), (own, 1), *pieces]

        def body(*refs):
            for at, ref in enumerate(refs[:-1]):
                refs[-1][pl.ds(at * half, half), :] = ref[...]

        def columns(at):
            return pl.BlockSpec((half, width // 4), lambda i: (at, i))

        even = shape_of(half * self.size, width)
        even = self.clock.call(
            body, [array for array, _ in pieces], [columns(at) for _, at in pieces],
            [even], [column_blocks(even.shape[0], width // 4)], 4, vmem=24,
        )[0]
        self.gathered = even, self.swap(even, 1)
        self.clock.pause(4)

    def stacked(self, outs, rows):
        terms = [term for out in outs for block in out for term in block]
        width = terms[0][0].shape[1]

        def body(*refs):
            ins = iter(refs[: len(terms)])
            for out, ref in zip(outs, refs[len(terms) :]):
                for at, block in enumerate(out):
                    values = [next(ins)[...] for _ in block]
                    if len(values) > 1:
                        values = [sum(v.astype(F32) for v in values).astype(BF16)]
                    ref[pl.ds(at * rows, rows), :] = values[0]

        shapes = [shape_of(len(out) * rows, width) for out in outs]
        return self.clock.call(
            body, [array for array, _ in terms], [row_block_at(rows, width, at) for _, at in terms],
            shapes, [whole_out(o) for o in shapes], vmem=40,
        )

    def partner(self, odd):
        if not self.fast:
            return odd
        other = self.swap(odd, 1)
        self.clock.pause(4)
        return other

    def ride(self, own):
        if self.fast:
            self.riding = self.swap(own, 2), self.swap(own, 4)
            self.clock.pause(1)

    def scatter(self, sets, own=None):
        if not self.fast:
            yield
            yield
            both = [jnp.concatenate(pair, 0) for pair in sets]
            totals = [lax.psum_scatter(b, "shard", scatter_dimension=0, tiled=True) for b in both]
            self.terms = [[[(total, 0)], [(total, 1)]] for total in totals]
            if own is not None:
                self.gather_all(own)
            return
        rows = sets[0][0].shape[0] // 8
        rider = self.clock.tie(*self.riding) if own is not None else None

        def both(pair, at):
            return [(pair[0], at), (pair[1], at)]

        to_x = [both(pair, at) for pair in sets for at in (3, 7)]
        to_y = [both(pair, at) for pair in sets for at in (4, 6)]
        to_x, to_y = self.stacked([to_x, to_y], rows)
        by_x, by_y = self.swap(to_x, 2), self.swap(to_y, 4)
        self.clock.pause(len(sets))
        yield
        count = len(sets)
        to_x = [both(pair, 2) + [(by_y, 2 * i + 1)] for i, pair in enumerate(sets)]
        to_y = [both(pair, 5) + [(by_x, 2 * i + 1)] for i, pair in enumerate(sets)]
        if rider:
            to_x.append([(rider[1], 1)])
            to_y.append([(rider[0], 0)])
        to_x, to_y = self.stacked([to_x, to_y], rows)
        last_x, last_y = self.swap(to_x, 2), self.swap(to_y, 4)
        self.clock.pause(0.6 * len(sets) + 0.4 * bool(rider))
        yield
        self.terms = [
            [
                both(pair, 0) + [(by_y, 2 * i), (last_x, i)],
                both(pair, 1) + [(by_x, 2 * i), (last_y, i)],
            ]
            for i, pair in enumerate(sets)
        ]
        if rider:
            first = [(rider[0], 0), (rider[0], 1), (rider[1], 0), (rider[1], 1)]
            self.rider = own, [*first, (last_y, count), (last_x, count)]

    def join_rider(self):
        if self.fast:
            self.join(*self.rider)

    def finish_rows(self, body, terms, args, outs):
        flat = [array for half in terms for array, _ in half]
        rows = args[0].shape[0] // 2
        columns = flat[0].shape[1]
        specs = [row_block_at(rows, columns, at) for half in terms for _, at in half]
        count = len(terms[0])

        def kernel(*refs):
            sums, rest = refs[: len(flat)], refs[len(flat) :]
            for half in (0, 1):
                total = sum(ref[...].astype(F32) for ref in sums[half * count : (half + 1) * count])
                body(pl.ds(half * rows, rows), total, *rest)

        return self.clock.call(
            kernel, [*flat, *args], [*specs, *[whole(a) for a in args]], outs,
            [whole_out(o) for o in outs], vmem=40,
        )

    def exchange(self, load, args, a, b, apart=False):
        smem = pl.BlockSpec(memory_space=pltpu.SMEM)
        specs = [smem, *[smem if v.ndim == 1 else whole(v) for v in args]]
        if not self.fast:

            def lay(me, *refs):
                for j in range(self.size):
                    refs[-1][j] = load(refs[:-1], j)

            every = jax.ShapeDtypeStruct((self.size, a, b), BF16)
            blocks = self.clock.call(lay, [self.me, *args], specs, [every], [whole_out(every)])[0]
            yield
            yield
            self.exchanged = lax.all_to_all(blocks, "shard", split_axis=0, concat_axis=0)
            return
        four, two = jax.ShapeDtypeStruct((4, a, b), BF16), jax.ShapeDtypeStruct((2, a, b), BF16)

        def pack(me, *refs):
            kept, sent = refs[-2:]
            for j in range(8):
                value = load(refs[:-2], j)
                k = me[0] ^ j

                @pl.when(k & 1 == 0)
                def _(value=value, k=k):
                    kept[k >> 1] = value

                @pl.when(k & 1 == 1)
                def _(value=value, k=k):
                    sent[k >> 1] = value

        kept, sent = self.clock.call(
            pack, [self.me, *args], specs, [four] * 2, [whole_out(four)] * 2, vmem=32
        )
        come = self.swap(sent, 1)
        mib = 8 * a * b / 2**20
        self.clock.pause(mib)
        yield

        def stack(kept, come, *outs):
            for i, out in enumerate(outs):
                out[0] = kept[i + 1]
                out[1] = come[i + 1]

        sends = self.clock.call(
            stack, [kept, come], [whole(kept), whole(come)], [two] * 3, [whole_out(two)] * 3, vmem=24
        )
        arrived = [self.swap(value, 2 * i + 2) for i, value in enumerate(sends[: 2 if apart else 3])]
        self.clock.pause(mib / 2)
        yield
        if apart:
            arrived.append(self.swap(self.clock.tie(sends[2]), 6))
            self.clock.pause(mib / 2)
            yield

        def unpack(me, kept, come, *rest):
            out = rest[-1]
            out[me[0]] = kept[0]
            out[me[0] ^ 1] = come[0]
            for i, ref in enumerate(rest[:-1]):
                out[me[0] ^ (2 * i + 2)] = ref[0]
                out[me[0] ^ (2 * i + 3)] = ref[1]

        eight = jax.ShapeDtypeStruct((8, a, b), BF16)
        first = pl.BlockSpec((1, a, b), lambda i: (0, 0, 0))
        self.exchanged = self.clock.call(
            unpack, [self.me, kept, come, *arrived], [smem, first, first, *[whole(v) for v in arrived]],
            [eight], [whole_out(eight)], vmem=24,
        )[0]


def drain(steps):
    for _ in steps:
        pass


class Attention:
    def __init__(self, clock, length, qcols, wqkv, wo):
        self.clock, self.length, self.qcols = clock, length, qcols
        self.wqkv, self.wo = wqkv, wo
        self.heads = qcols // HEAD_SIZE
        self.width = qcols + 2 * HEAD_SIZE
        half = HEAD_SIZE // 2
        freqs = 1.0 / 10000.0 ** (np.arange(half, dtype=np.float32) * 2.0 / HEAD_SIZE)
        angles = np.arange(length, dtype=np.float32)[:, None] * freqs[None, :].astype(np.float32)
        turns = self.heads + 1
        low = np.arange(turns * HEAD_SIZE) % HEAD_SIZE < half
        cosine = np.tile(np.cos(angles), (1, 2 * turns))
        sine = np.tile(np.sin(angles), (1, 2 * turns))
        plain = np.zeros((length, HEAD_SIZE), np.float32)
        self.tables = tuple(
            jnp.asarray(np.concatenate(pair, 1), F32)
            for pair in (
                (cosine, plain + 1.0),
                (np.where(low, -sine, 0.0), plain),
                (np.where(low, 0.0, sine), plain),
            )
        )

    def roll(self, value, by):
        return pltpu.roll(value, by % value.shape[1], 1)

    def stack(self, value):
        head = lax.broadcasted_iota(jnp.int32, value.shape, 1) // HEAD_SIZE
        return jnp.concatenate([jnp.where(head == h, value, 0.0) for h in range(self.heads)], 0).astype(BF16)

    def unstack(self, value):
        head = lax.broadcasted_iota(jnp.int32, (self.length, self.qcols), 1) // HEAD_SIZE
        total = jnp.zeros((self.length, self.qcols), F32)
        for h in range(self.heads):
            total = jnp.where(head == h, value[h * self.length : (h + 1) * self.length], total)
        return total

    def repeated(self, value):
        first = lax.broadcasted_iota(jnp.int32, value.shape, 1) < HEAD_SIZE
        turned = self.roll(value, HEAD_SIZE)
        times = self.qcols // (2 * HEAD_SIZE)
        key = jnp.where(first, value, turned).astype(BF16)
        val = jnp.where(first, turned, value).astype(BF16)
        return jnp.concatenate([key] * times, 1), jnp.concatenate([val] * times, 1)

    def probabilities(self, stacked, keys):
        raw = dot_nt(stacked, keys) * (1.0 / math.sqrt(HEAD_SIZE))
        raw = raw.reshape(self.heads, self.length, self.length)
        at = lax.broadcasted_iota(jnp.int32, raw.shape, 1)
        seen = lax.broadcasted_iota(jnp.int32, raw.shape, 2) <= at
        scores = jnp.where(seen, raw, -1e30)
        e = jnp.exp(scores - jnp.max(scores, -1, keepdims=True))
        prob = e / jnp.sum(e, -1, keepdims=True)
        return prob.reshape(self.heads * self.length, self.length)

    def forward(self, tokens):
        rows, width = tokens.shape
        block, length, qcols = 2 * self.length, self.length, self.qcols

        def body(x, wqkv, wo, c, s1, s2, qkv_out, inv_out, context_t, partial_out):
            source = x[...].astype(F32)
            inv = lax.rsqrt(jnp.mean(source * source, -1, keepdims=True) + EPS)
            inv_out[...] = jnp.broadcast_to(inv, (block, 128))
            lin = dot(x[...], wqkv[...]) * inv
            contexts = []
            for at in range(0, block, length):
                v = lin[at : at + length]
                v = v * c[...] + self.roll(v, -32) * s1[...] + self.roll(v, 32) * s2[...]
                v = v.astype(BF16).astype(F32)
                qkv_out[pl.ds(at, length), :] = v.astype(BF16)
                keys, values = self.repeated(v[:, qcols:])
                prob = self.probabilities(self.stack(v[:, :qcols]), keys)
                context = self.unstack(dot(prob.astype(BF16), values))
                contexts.append(context.astype(BF16))
            context = jnp.concatenate(contexts, 0)
            context_t[...] = context.T
            partial_out[...] = dot(context, wo[...]).astype(BF16)

        args = (tokens, self.wqkv, self.wo, *self.tables)
        return self.clock.call(
            body, args, [row_blocks(block, width), *[whole(a) for a in args[1:]]],
            [shape_of(rows, self.width), shape_of(rows, 128, F32), shape_of(qcols, rows), shape_of(rows, width)],
            [
                row_blocks(block, self.width),
                row_blocks(block, 128),
                column_blocks(qcols, block),
                row_blocks(block, width),
            ],
            rows // block,
        )

    def backward(self, grad, qkv, inv):
        rows, width = grad.shape
        block, length, qcols = 2 * self.length, self.length, self.qcols
        scale = 1.0 / math.sqrt(HEAD_SIZE)

        def fold(value):
            folded = sum(value[:, i : i + 2 * HEAD_SIZE] for i in range(0, qcols, 2 * HEAD_SIZE))
            return folded + self.roll(folded, HEAD_SIZE)

        def body(d, qkv_in, inv_in, wqkv, wo, c, s1, s2, grad_t, partial_out):
            grads = []
            dcontext = dot_nt(d[...], wo[...]).astype(BF16).astype(F32)
            for at in range(0, block, length):
                v = qkv_in[pl.ds(at, length), :].astype(F32)
                keys, values = self.repeated(v[:, qcols:])
                stacked = self.stack(v[:, :qcols])
                prob = self.probabilities(stacked, keys)
                dstacked = self.stack(dcontext[at : at + length])
                dprob = dot_nt(dstacked, values)
                dvalue = fold(dot_tn(prob.astype(BF16), dstacked))
                ds = prob * (dprob - jnp.sum(prob * dprob, -1, keepdims=True))
                ds = ds.astype(BF16)
                dq = self.unstack(dot(ds, keys)) * scale
                dkey = fold(dot_tn(ds, stacked)) * scale
                first = lax.broadcasted_iota(jnp.int32, dkey.shape, 1) < HEAD_SIZE
                g = jnp.concatenate([dq, jnp.where(first, dkey, dvalue)], 1)
                g = g * c[...] - self.roll(g, -32) * s1[...] - self.roll(g, 32) * s2[...]
                grads.append(g)
            g = jnp.concatenate(grads, 0)
            grad_t[...] = (g * inv_in[:, :1]).astype(BF16).T
            partial_out[...] = dot_nt(g.astype(BF16), wqkv[...]).astype(BF16)

        args = (grad, qkv, inv, self.wqkv, self.wo, *self.tables)
        return self.clock.call(
            body, args,
            [
                row_blocks(block, width),
                row_blocks(block, self.width),
                row_blocks(block, 128),
                *[whole(a) for a in args[3:]],
            ],
            [shape_of(self.width, rows), shape_of(rows, width)],
            [column_blocks(self.width, block), row_blocks(block, width)],
            rows // block,
        )


def feed(clock, normed, dy, wg, wu, wd, block=256):
    rows, width = normed.shape
    ff = wd.shape[0]

    def body(x, d, wg, wu, wd, act_out, dgate_out, dup_out, act_t, dgate_t, dup_t):
        gate = dot(x[...], wg[...])
        up = dot(x[...], wu[...])
        dact = dot_nt(d[...], wd[...])
        sigma = jax.nn.sigmoid(gate)
        silu = gate * sigma
        act = (silu * up).astype(BF16)
        dgate = (dact * up * (sigma * (1.0 + gate * (1.0 - sigma)))).astype(BF16)
        dup = (dact * silu).astype(BF16)
        for value, out, turned in ((act, act_out, act_t), (dgate, dgate_out, dgate_t), (dup, dup_out, dup_t)):
            out[...] = value
            turned[...] = value.T

    args = (normed, dy, wg, wu, wd)
    return clock.call(
        body, args, [row_blocks(block, width)] * 2 + [whole(a) for a in args[2:]],
        [shape_of(rows, ff)] * 3 + [shape_of(ff, rows)] * 3,
        [row_blocks(block, ff)] * 3 + [column_blocks(ff, block)] * 3,
        rows // block,
    )


def assemble(clock, me, above, below):
    copies = len(above)
    a, _, b, c = above[0].shape

    def body(me_ref, *refs):
        outs = refs[2 * copies - 1 :]
        for step in range(copies):
            at = lax.rem(me_ref[0] + step, copies)

            def store(ref, at=at):
                for which, out in enumerate(outs):
                    out[0, at] = ref[0, which]

            if step == 0:
                store(refs[0])
                continue

            @pl.when(me_ref[0] + step < copies)
            def _(ref=refs[copies + step - 1], store=store):
                store(ref)

            @pl.when(me_ref[0] + step >= copies)
            def _(ref=refs[copies - step], store=store):
                store(ref)

    args = [*above, *below[1:]]
    out = jax.ShapeDtypeStruct((a, copies, b, c), BF16)
    spec = pl.BlockSpec((1, 2, b, c), lambda i: (i, 0, 0, 0))
    out_spec = pl.BlockSpec((1, copies, b, c), lambda i: (i, 0, 0, 0))
    me = jnp.asarray(me, jnp.int32).reshape(1)
    return clock.call(
        body, [me, *args], [pl.BlockSpec(memory_space=pltpu.SMEM)] + [spec] * len(args),
        [out] * 2, [out_spec] * 2, a, vmem=24,
    )


def feed_weight_grad(clock, parts, weight, gain):
    own, columns = weight.shape
    shards = parts[0].shape[0]
    ff = sum(part.shape[1] for part in parts)
    join = 128 // math.gcd(ff, 128)

    def body(*refs):
        (w, g, grad_out, sum_out), ins = refs[len(parts) :], refs[: len(parts)]
        value = jnp.concatenate([ref[...] for ref in ins], 1) if len(ins) > 1 else ins[0][...]
        value = value.reshape(join * ff, own).astype(F32).T * g[...]
        grad_out[...] = value

        @pl.when(pl.program_id(0) == 0)
        def _():
            sum_out[...] = jnp.zeros_like(sum_out)

        total = jnp.sum(w[...].astype(F32) * value, -1, keepdims=True)
        sum_out[...] += jnp.broadcast_to(total, sum_out.shape)

    specs = [pl.BlockSpec((join, part.shape[1], own), lambda i: (i, 0, 0)) for part in parts]
    total = shape_of(own, 128, F32)
    return clock.call(
        body, [*parts, weight, gain], [*specs, column_blocks(own, join * ff), whole(gain)],
        [shape_of(own, columns, F32), total], [column_blocks(own, join * ff), whole_out(total)], shards // join,
    )


def qkv_weight_grad(clock, part, wq, wk, wv, gain):
    shards, cols, own = part.shape
    qcols, kv = wq.shape[1] // shards, wk.shape[1]
    sharing = shards * HEAD_SIZE // kv

    def body(ins, wq, wk, wv, g, q_out, k_out, v_out, sum_out):
        total = jnp.zeros((own, 1), F32)
        tails = []
        for j in range(shards):
            value = ins[j].astype(F32).T * g[...]
            at = pl.ds(j * qcols, qcols)
            q_out[:, at] = value[:, :qcols]
            total += jnp.sum(wq[:, at].astype(F32) * value[:, :qcols], -1, keepdims=True)
            tails.append(value[:, qcols:])
        tails = [sum(tails[j : j + sharing]) for j in range(0, shards, sharing)]
        for w, out, at in ((wk, k_out, 0), (wv, v_out, HEAD_SIZE)):
            value = jnp.concatenate([tail[:, at : at + HEAD_SIZE] for tail in tails], 1)
            out[...] = value
            total += jnp.sum(w[...].astype(F32) * value, -1, keepdims=True)
        sum_out[...] = jnp.broadcast_to(total, (own, 128))

    args = [part, wq, wk, wv, gain]
    outs = [shape_of(own, n, F32) for n in (shards * qcols, kv, kv, 128)]
    return clock.call(body, args, [whole(a) for a in args], outs, [whole_out(o) for o in outs])


def widen(clock, value, start, rows, at=0, pieces=1, into=None):
    width = value.shape[1]

    def body(ref, *rest):
        rest[-1][...] = ref[start : start + rows, :].astype(F32)

    return clock.call(
        body, [value] + ([into] if into is not None else []),
        [column_blocks(value.shape[0], width // 4)] + ([TOKEN] if into is not None else []),
        [shape_of(pieces * rows, width, F32)], [pl.BlockSpec((rows, width // 4), lambda i: (at, i))], 4,
        aliases={1: 0} if into is not None else None,
    )[0]


def product(clock, lefts, rights, turned, block=512):
    rows = lefts[0].shape[0]
    width = rights[0].shape[0 if turned else 1]
    count = len(lefts)

    def body(*refs):
        pairs = zip(refs[:count], refs[count : 2 * count])
        multiply = dot_nt if turned else dot
        refs[-1][...] = sum(multiply(a[...], b[...]) for a, b in pairs).astype(BF16)

    return clock.call(
        body, [*lefts, *rights],
        [row_blocks(block, a.shape[1]) for a in lefts] + [whole(b) for b in rights],
        [shape_of(rows, width)], [row_blocks(block, width)], rows // block,
    )[0]


def weight_grad(clock, lefts, rights, cuts, at=0, above=None, padding=0, block=512):
    rows = sum(cuts)
    width = rights[0].shape[1]
    count = len(lefts)
    extra = [above] if above is not None else []
    heights = list(cuts)
    heights[-1] += padding + sum(v.shape[0] for v in extra)

    def body(*refs):
        lefts, rights, outs = refs[:count], refs[count : 2 * count], refs[2 * count + len(extra) :]
        total = sum(dot(a[...], b[...]) for a, b in zip(lefts, rights)).astype(BF16)
        parts = [ref[...] for ref in refs[2 * count : 2 * count + len(extra)]] + [total]
        if padding:
            parts.append(jnp.zeros((padding, block), BF16))
        total = jnp.concatenate(parts, 0) if len(parts) > 1 else total
        start = 0
        for height, out in zip(heights, outs):
            out[...] = total[start : start + height]
            start += height

    def left(array):
        return pl.BlockSpec((rows, array.shape[1]), lambda i: (at, 0), pipeline_mode=pl.Buffered(1))

    return clock.call(
        body, [*lefts, *rights, *extra],
        [left(a) for a in lefts] + [column_blocks(b.shape[0], block) for b in [*rights, *extra]],
        [shape_of(height, width) for height in heights],
        [column_blocks(height, block) for height in heights], width // block,
    )


def on_device(shards, copies, tokens, gain1, wq, wk, wv, wo, gain2, wg, wu, wd, out_grad):
    seqs, length, width = tokens.shape
    rows = seqs * length
    clock = Clock()
    group, line = Group(shards, clock), Line(copies, clock)
    kv_heads = wk.shape[1] // HEAD_SIZE
    sharing = shards // kv_heads
    ff, qcols, own = wd.shape[0], wo.shape[0], wq.shape[0]
    cols = qcols + 2 * HEAD_SIZE
    g1 = gain1.astype(F32)[:, None]
    g2 = gain2.astype(F32)[:, None]
    flat = tokens.reshape(rows, width)
    low = out_grad.reshape(rows, width)

    x_steps = group.gather(flat)
    next(x_steps)

    def load_qkv(refs, j):
        wq, wk, wv, g = refs
        head = j // sharing * HEAD_SIZE
        parts = wq[:, j * qcols : (j + 1) * qcols], wk[:, head : head + HEAD_SIZE], wv[:, head : head + HEAD_SIZE]
        return (jnp.concatenate([p.astype(F32) for p in parts], 1) * g[...]).astype(BF16)

    qkv_steps = group.exchange(load_qkv, [wq, wk, wv, g1], own, cols)
    next(qkv_steps)
    next(x_steps)
    next(qkv_steps)

    share = own // copies

    def load_feed(refs, j):
        copy, wg, wu, g = refs
        at = pl.ds(pl.multiple_of(copy[0] * share, share), share)
        parts = [w[at, j * ff : (j + 1) * ff].astype(F32) * g[at, :] for w in (wg, wu)]
        return jnp.concatenate(parts, 0).astype(BF16)

    copy = jnp.asarray(line.me, jnp.int32).reshape(1)
    feed_steps = group.exchange(load_feed, [copy, wg, wu, g2], 2 * share, ff)
    next(feed_steps)
    drain(x_steps)
    x_all = group.gathered
    drain(qkv_steps)
    wqkv = group.exchanged.reshape(width, cols)
    next(feed_steps)

    attention = Attention(clock, length, qcols, wqkv, wo)
    qkv_o, inv_o, context_ot, part_o = attention.forward(x_all[1])
    other = group.partner(part_o)
    drain(feed_steps)
    share_steps = line.share(group.exchanged.reshape(shards, 2, share, ff))
    next(share_steps, None)
    group.ride(clock.tie(low))
    qkv_e, inv_e, context_et, part_e = attention.forward(x_all[0])
    h1_steps = group.scatter([(part_e, other)], low)
    next(h1_steps)
    next(share_steps, None)
    next(h1_steps)
    next(share_steps, None)
    drain(h1_steps)

    def first_half(at, total, x, h1, inv2, n2):
        value = x[at, :].astype(F32) + total
        inv = lax.rsqrt(jnp.mean(value * value, -1, keepdims=True) + EPS)
        h1[at, :] = value
        inv2[at, :] = jnp.broadcast_to(inv, (inv.shape[0], 128))
        n2[at, :] = (value * inv).astype(BF16)

    h1, inv2, n2 = group.finish_rows(
        first_half, group.terms[0], [flat], [shape_of(rows, width, F32), shape_of(rows, 128, F32), shape_of(rows, width)]
    )
    n2_steps = group.gather(n2)
    next(n2_steps)
    group.join_rider()
    dy = group.gathered
    next(n2_steps)
    drain(share_steps)
    wg_mine, wu_mine = assemble(clock, line.me, *line.shared)
    wg_mine, wu_mine = wg_mine.reshape(width, ff), wu_mine.reshape(width, ff)
    drain(n2_steps)
    n2 = group.gathered
    results = {}

    def sum_copies(name, parts, first=0):
        for at, part in enumerate(parts, first):
            line.queue(part, functools.partial(results.__setitem__, (name, at)))

    def exchange_back(*parts):
        def load(refs, j):
            blocks = [ref[:rows, j * own : (j + 1) * own] for ref, (_, rows) in zip(refs, parts)]
            return jnp.concatenate(blocks, 0) if len(blocks) > 1 else blocks[0]

        return group.exchange(load, [value for value, _ in parts], sum(rows for _, rows in parts), own)

    piece = ff // 2
    rest = cols - piece
    padding = piece - rest - qcols
    if line.size != 4 or rest < 0 or padding < 0:
        rest = padding = 0

    act_e, dgate_e, dup_e, act_et, dgate_et, dup_et = feed(clock, n2[0], dy[0], wg_mine, wu_mine, wd)
    act_o, dgate_o, dup_o, act_ot, dgate_ot, dup_ot = feed(clock, n2[1], dy[1], wg_mine, wu_mine, wd)
    down_parts = weight_grad(clock, (act_et, act_ot), dy, [piece, piece])
    sum_copies("down", down_parts[:1])
    line.tick()
    sum_copies("gate", weight_grad(clock, (dgate_et, dgate_ot), n2, [piece]))
    other = group.partner(product(clock, (dgate_o, dup_o), (wg_mine, wu_mine), True))
    part_e = product(clock, (dgate_e, dup_e), (wg_mine, wu_mine), True)
    a2_steps = group.scatter([(part_e, other)])
    next(a2_steps)
    line.tick()
    sum_copies("gate", weight_grad(clock, (dgate_et, dgate_ot), n2, [piece], at=1), 1)
    sum_copies("up", weight_grad(clock, (dup_et, dup_ot), n2, [piece, piece]))
    next(a2_steps)
    line.tick()
    drain(a2_steps)

    def second_half(at, total, dy, h1, inv2, dh1, low_out):
        value, inv = h1[at, :], inv2[at, :1]
        middle = jnp.mean(total * value, -1, keepdims=True)
        grad = dy[at, :].astype(F32) + inv * total - value * (inv * inv * inv) * middle
        dh1[at, :] = grad
        low_out[at, :] = grad.astype(BF16)

    dh1, dattn = group.finish_rows(
        second_half, group.terms[0], [low, h1, inv2], [shape_of(rows, width, F32), shape_of(rows, width)]
    )
    dattn_steps = group.gather(dattn)
    next(dattn_steps)
    out_parts = product(clock, (act_e,), (wd,), False), group.partner(product(clock, (act_o,), (wd,), False))
    next(dattn_steps)
    line.tick()
    drain(dattn_steps)
    dattn = group.gathered
    dqkv_et, part_e = attention.backward(dattn[0], qkv_e, inv_e)
    dqkv_ot, part_o = attention.backward(dattn[1], qkv_o, inv_o)
    other = group.partner(part_o)
    line.tick()
    a1_steps = group.scatter([(part_e, other), out_parts])
    next(a1_steps)
    qkv_pieces = weight_grad(clock, (dqkv_et, dqkv_ot), x_all, [cols - rest] + [rest] * (rest > 0))
    sum_copies("qkv", qkv_pieces[:1])
    above = qkv_pieces[1] if rest else None
    context_t = context_et, context_ot
    sum_copies("o", weight_grad(clock, context_t, dattn, [qcols], above=above, padding=padding))
    sum_copies("down", down_parts[1:], 1)
    line.tick()
    next(a1_steps)
    line.tick()
    drain(a1_steps)

    def output(at, total, h1, out):
        out[at, :] = (h1[at, :] + total).astype(BF16)

    def input_half(at, total, x, dh1, out):
        value = x[at, :].astype(F32)
        inv = lax.rsqrt(jnp.mean(value * value, -1, keepdims=True) + EPS)
        middle = jnp.mean(total * value, -1, keepdims=True)
        out[at, :] = dh1[at, :] + inv * total - value * (inv * inv * inv) * middle

    (input_grad,) = group.finish_rows(
        input_half, group.terms[0], [flat, dh1], [shape_of(rows, width, F32)]
    )
    (layer_out,) = group.finish_rows(output, group.terms[1], [h1], [shape_of(rows, width)])
    def tick_until(name, at):
        while (name, at) not in results:
            line.tick(0.1)

    tick_until("gate", 1)
    gate_steps = exchange_back((results["gate", 0], piece), (results["gate", 1], piece))
    next(gate_steps)
    tick_until("up", 1)
    next(gate_steps)
    down_grad = widen(clock, results["down", 0], 0, piece, 0, 2)
    up_steps = exchange_back((results["up", 0], piece), (results["up", 1], piece))
    next(up_steps)
    tick_until("qkv", 0)
    drain(gate_steps)
    gate_back = group.exchanged
    next(up_steps)
    gate_grad, gate_sums = feed_weight_grad(clock, [gate_back], wg, g2)
    tick_until("o", 0)
    qkv_steps = exchange_back((results["qkv", 0], cols - rest), *[(results["o", 0], rest)] * (rest > 0))
    next(qkv_steps)
    drain(up_steps)
    up_back = group.exchanged
    next(qkv_steps)
    o_grad = widen(clock, results["o", 0], rest, qcols)
    up_grad, up_sums = feed_weight_grad(clock, [up_back], wu, g2)
    drain(qkv_steps)
    q_grad, k_grad, v_grad, qkv_sums = qkv_weight_grad(clock, group.exchanged, wq, wk, wv, g1)
    tick_until("down", 1)
    down_grad = widen(clock, results["down", 1], 0, piece, 1, 2, down_grad)

    gain1_grad = qkv_sums[:, 0] / g1[:, 0]
    gain2_grad = (gate_sums[:, 0] + up_sums[:, 0]) / g2[:, 0]
    return (
        layer_out.reshape(seqs, length, width),
        input_grad.reshape(seqs, length, width),
        gain1_grad,
        q_grad,
        k_grad,
        v_grad,
        o_grad,
        gain2_grad,
        gate_grad,
        up_grad,
        down_grad,
    )


def solution(mesh):
    rows = P(("shard", "rep"), None, None)
    vector, matrix = P("shard"), P("shard", None)
    return jax.shard_map(
        functools.partial(on_device, mesh.shape["shard"], mesh.shape["rep"]),
        mesh=mesh,
        in_specs=(rows, vector, matrix, matrix, matrix, matrix, vector, matrix, matrix, matrix, rows),
        out_specs=(rows, rows, vector, matrix, matrix, matrix, matrix, vector, matrix, matrix, matrix),
        check_vma=False,
    )
```
